512 devices in a mesh: dp: 32 (over x, y, core), fsdp: 16 (over z).
Axes of the slice: x: 4, y: 4, z: 16, core: 2. Of those that a mesh axis runs over, the one named last changes fastest.
Arguments:
- tokens: bfloat16 [65536, 8192], P(('dp', 'fsdp')), may hold values from -6 to 6
- weight: bfloat16 [8192, 384], P('fsdp'), may hold values from -0.0625 to 0.0625
- target: bfloat16 [65536, 384], P(('dp', 'fsdp')), may hold values from -6 to 6
- bounds: int32 [16, 32, 2], P('fsdp', 'dp'), may hold values from 0 to 64, as said below
- kept: int32 [32, 16, 40], P('dp', 'fsdp'), may hold values from 0 to 63, as said below
Outputs:
- inputs_grad: bfloat16 [65536, 8192], P(('dp', 'fsdp'))
- selected: bfloat16 [8192, 384], P('fsdp')
- owned_tiles: float32 [16, 32, 3, 3072], P('fsdp', 'dp')
The draws below stay inside these ranges and needn't reach their ends.
Inputs may be any that keep to these rules, and one draw needn't show every extreme that they name: For each shard, owner r's region is tiles bounds[., r, 0] to bounds[., r, 1] - 1; consecutive owners have consecutive regions covering all 64 tiles; each region holds 1 to 3 tiles and some region exactly 3. `kept`: each list holds 40 distinct tile indices; in every shard some replica keeps every tile of a region of 3 tiles.
All inputs are finite; a program needn't handle non-finite values.
Results may differ from the reference program's by a relative error of at most 0.011.
Values may be sent and summed in bfloat16 or wider, within the bound.
No kernel may reach another device: no remote copies, remote signals or barrier semaphores. Data moves between devices by JAX's collectives and lax.ppermute only.
A program may use at most 64 MiB of HBM per device.

```python
import math
import jax
import jax.numpy as jnp
from jax import lax

D = 8192
E = 384
TOK_DEV = 128
TILE_ROWS = 8
TILE_COLS = 384
TOKENS = 65536
TILES = 64
MAXREG = 3
KEEP = 40
N_DP = 32
N_FSDP = 16


def region_sizes(key):
    base_size = TILES // N_DP
    half_size = base_size // 2
    pair_count = N_DP // 2
    key_wobble, key_order = jax.random.split(key)
    wobble = jax.random.randint(key_wobble, (N_FSDP, pair_count), 0, half_size + 1)
    wobble = wobble.at[:, 0].set(half_size)
    region_len = jnp.concatenate([base_size + wobble, base_size - wobble], axis=1)
    row_keys = jax.random.split(key_order, N_FSDP)
    shuffle = jax.vmap(lambda one_key: jax.random.permutation(one_key, N_DP))(row_keys)
    return jnp.take_along_axis(region_len, shuffle, axis=1).astype(jnp.int32)


def draw_bounds(key, part):
    region_len = region_sizes(key)
    region_end = jnp.cumsum(region_len, axis=1).astype(jnp.int32)
    region_start = region_end - region_len
    return jnp.stack([region_start, region_end], axis=-1).astype(jnp.int32)


def draw_kept(key, part):
    region_len = region_sizes(key)
    key = jax.random.fold_in(key, 7)
    region_end = jnp.cumsum(region_len, axis=1).astype(jnp.int32)
    region_start = region_end - region_len
    largest = jnp.argmax(region_len, axis=1)
    big_start = jnp.take_along_axis(region_start, largest[:, None], axis=1)
    key_perm, key_who = jax.random.split(key)
    row_keys = jax.random.split(key_perm, N_DP * N_FSDP)
    ranking = jax.vmap(lambda one_key: jax.random.permutation(one_key, TILES))(row_keys).reshape(N_DP, N_FSDP, TILES)
    chooser = jax.random.randint(key_who, (N_FSDP,), 0, N_DP)
    tile_ids = jnp.arange(TILES, dtype=jnp.int32)
    in_big = (tile_ids[None, :] >= big_start) & (tile_ids[None, :] < big_start + MAXREG)
    picked = jnp.arange(N_DP, dtype=jnp.int32)[:, None] == chooser[None, :]
    boost = (picked[:, :, None] & in_big[None, :, :]).astype(jnp.int32)
    scores = ranking.astype(jnp.int32) - TILES * boost
    ordering = jnp.argsort(scores, axis=-1, stable=True)
    return ordering[..., :KEEP].astype(jnp.int32)


def levels(own_key, dims, pieces, smallest, high):
    def one(axis_at, blocks):
        draws = jax.random.uniform(jax.random.fold_in(jax.random.fold_in(own_key, 6), axis_at), (blocks,), jnp.float32, smallest / len(pieces), high / len(pieces))
        return jnp.repeat(jnp.exp(draws), dims[axis_at] // blocks).reshape((-1,) + (1,) * (len(dims) - axis_at - 1))

    gain = one(*pieces[0])
    for cut in pieces[1:]:
        gain = gain * one(*cut)
    return gain


def bell_draw(rng, dims, scale, bound, shards=(), kind=jnp.bfloat16):
    gain = levels(rng, dims, shards, -0.22, 0.18) if shards else 1.0
    entries = jax.random.normal(rng, dims, jnp.float32) * scale * gain
    return jnp.minimum(jnp.maximum(entries, -bound), bound).astype(kind)


def setup_inputs(seed: int = 0) -> dict:
    key_of = jax.random.split(jax.random.key(seed), 6)
    return {
        "tokens": bell_draw(key_of[0], (TOKENS, D), 1.0, 6.0, ((0, 512),)),
        "weight": bell_draw(key_of[1], (D, E), D ** -0.5, 0.0625, ((0, 16),)),
        "target": bell_draw(key_of[2], (TOKENS, E), 1.0, 6.0, ((0, 512),)),
        "bounds": draw_bounds(jax.random.fold_in(key_of[5], 71), 0),
        "kept": draw_kept(jax.random.fold_in(key_of[5], 71), 0),
    }


def make_tiles(shard_grad):
    blocks = shard_grad.reshape(N_FSDP, D // N_FSDP // TILE_ROWS, TILE_ROWS, E // TILE_COLS, TILE_COLS)
    return blocks.transpose(0, 1, 3, 2, 4).reshape(N_FSDP, TILES, TILE_ROWS * TILE_COLS)

def reference(tokens, weight, target, bounds, kept):
    outputs = jnp.dot(tokens, weight, preferred_element_type=jnp.float32)
    errors = (outputs - target).astype(jnp.bfloat16)
    inputs_grad = jnp.dot(errors, weight.T, preferred_element_type=jnp.float32).astype(jnp.bfloat16)
    rep_tokens = TOK_DEV * N_FSDP
    grad_scale = 1.0 / math.sqrt(rep_tokens * N_DP)
    tile_ids = jnp.arange(TILES, dtype=jnp.int32)
    hit_mask = jnp.any(kept[..., None] == tile_ids, axis=2)

    def accumulate(running, inputs):
        replica, hits = inputs
        block_in = lax.dynamic_slice_in_dim(tokens, (replica * rep_tokens).astype(jnp.int32), rep_tokens, 0)
        block_err = lax.dynamic_slice_in_dim(errors, (replica * rep_tokens).astype(jnp.int32), rep_tokens, 0)
        shard_grad = jnp.dot(block_in.T, block_err, preferred_element_type=jnp.float32) * grad_scale
        masked = jnp.where(hits[..., None], make_tiles(shard_grad), 0.0)
        return (running + masked, None)
    zeroes = jnp.zeros((N_FSDP, TILES, TILE_ROWS * TILE_COLS), jnp.float32)
    dense_tiles, _ = lax.scan(accumulate, zeroes, (jnp.arange(N_DP, dtype=jnp.int32), hit_mask))
    blocks = dense_tiles.reshape(N_FSDP, D // N_FSDP // TILE_ROWS, E // TILE_COLS, TILE_ROWS, TILE_COLS)
    selected = blocks.transpose(0, 1, 3, 2, 4).reshape(D, E).astype(jnp.bfloat16)
    region_start = bounds[..., 0]
    region_len = bounds[..., 1] - region_start
    slot_ids = jnp.arange(MAXREG, dtype=jnp.int32)
    position = jnp.clip(region_start[..., None] + slot_ids, 0, TILES - 1).reshape(N_FSDP, N_DP * MAXREG)
    gathered = jnp.take_along_axis(dense_tiles, position[..., None], axis=1)
    valid = slot_ids < region_len[..., None]
    owned_tiles = jnp.where(valid[..., None], gathered.reshape(N_FSDP, N_DP, MAXREG, TILE_ROWS * TILE_COLS), 0.0)
    return (inputs_grad, selected, owned_tiles)
```

```python
import functools
import math

import jax
import jax.numpy as jnp
from jax import lax
from jax.experimental import pallas as pl
from jax.experimental.pallas import tpu as pltpu
from jax.sharding import Mesh, PartitionSpec as P

TILE_ROWS = 8
NX, NY, NC, NZ = 4, 4, 2, 16
PLANE = NX * NY
OWNERS = PLANE * NC
F32, BF16 = jnp.float32, jnp.bfloat16
VMEM_LIMIT = 48 * 1024 * 1024


def cut_kernel(tok_ref, out_ref):
    turned = tok_ref[...].T
    out_ref[...] = turned.reshape(out_ref.shape)


def cut_tokens(tokens):
    count, width = tokens.shape
    rows = width // NZ
    part = rows // PLANE
    return pl.pallas_call(
        cut_kernel,
        grid=(NZ,),
        in_specs=[pl.BlockSpec((count, rows), lambda j: (0, j))],
        out_specs=pl.BlockSpec((PLANE, 1, part, count), lambda j: (0, j, 0, 0)),
        out_shape=jax.ShapeDtypeStruct((PLANE, NZ, part, count), tokens.dtype),
        compiler_params=pltpu.CompilerParams(vmem_limit_bytes=VMEM_LIMIT),
        cost_estimate=pl.CostEstimate(flops=0, bytes_accessed=4 * count * width, transcendentals=0),
        name="cut_tokens",
    )(tokens)


def grad_kernel(scale, feat_ref, err_ref, mask_ref, out_ref, total):
    step = pl.program_id(0)
    pair = feat_ref.shape[0]
    rows, count = feat_ref.shape[1], feat_ref.shape[2]

    @pl.when(step == 0)
    def _():
        total[...] = jnp.zeros_like(total)

    kept = [
        feat_ref[p] * jnp.broadcast_to(mask_ref[0, :, p : p + 1], (rows, count)).astype(BF16)
        for p in range(pair)
    ]
    total[...] += jnp.dot(
        jnp.concatenate(kept, axis=1),
        err_ref[...].reshape(pair * count, err_ref.shape[2]),
        preferred_element_type=F32,
    )

    @pl.when(step == pl.num_programs(0) - 1)
    def _():
        done = (total[...] * scale).astype(BF16).reshape(NZ, NC, -1, out_ref.shape[-1])
        for c in range(NC):
            out_ref[c] = done[:, c]


def grad_parts(features, errors, mask, scale):
    members, rows, count = features.shape
    width = errors.shape[2]
    pair = 2
    return pl.pallas_call(
        functools.partial(grad_kernel, scale),
        grid=(members // pair,),
        in_specs=[
            pl.BlockSpec((pair, rows, count), lambda i: (i, 0, 0)),
            pl.BlockSpec((pair, count, width), lambda i: (i, 0, 0)),
            pl.BlockSpec((1, rows, pair), lambda i: (i, 0, 0)),
        ],
        out_specs=pl.BlockSpec((NC, NZ, rows // (NC * NZ), width), lambda i: (0, 0, 0, 0)),
        out_shape=jax.ShapeDtypeStruct((NC, NZ, rows // (NC * NZ), width), BF16),
        scratch_shapes=[pltpu.VMEM((rows, width), F32)],
        compiler_params=pltpu.CompilerParams(vmem_limit_bytes=VMEM_LIMIT),
        cost_estimate=pl.CostEstimate(
            flops=2 * members * rows * count * width,
            bytes_accessed=2 * members * count * (rows + width),
            transcendentals=0,
        ),
        name="grad_parts",
    )(features, errors, mask)


def sum_kernel(parts_ref, out_ref):
    total = jnp.sum(parts_ref[...].astype(F32), axis=0).astype(BF16)
    out_ref[...] = jnp.broadcast_to(total[None], out_ref.shape)


def sum_and_copy(parts, copies):
    return pl.pallas_call(
        sum_kernel,
        out_shape=jax.ShapeDtypeStruct((copies, *parts.shape[1:]), BF16),
        compiler_params=pltpu.CompilerParams(vmem_limit_bytes=VMEM_LIMIT),
        name="sum_and_copy",
    )(parts)


def exchange(parts, axes):
    return lax.all_to_all(parts, axes, split_axis=0, concat_axis=0, tiled=True)


def body(tokens, weight, target, bounds, kept):
    count, model = tokens.shape
    shard_rows, width = weight.shape
    tiles = shard_rows // TILE_ROWS
    share = tiles // PLANE
    scale = 1.0 / math.sqrt(count * NZ * OWNERS)

    whole = lax.all_gather(weight, "z", axis=0, tiled=True)

    hits = jnp.any(kept.reshape(-1, 1) == jnp.arange(tiles, dtype=jnp.int32), axis=0)
    hits = jnp.broadcast_to(hits.astype(F32), (NZ, 1, tiles))
    hits = exchange(hits, "z").reshape(NZ, PLANE, share).transpose(1, 0, 2)
    features = exchange(cut_tokens(tokens), ("x", "y"))
    hits = exchange(hits.reshape(PLANE, 1, NZ * share), ("x", "y"))
    mask = jnp.repeat(hits.reshape(PLANE // 2, 2, NZ * share), TILE_ROWS, axis=2).transpose(0, 2, 1)
    features = features.reshape(PLANE, model // PLANE, count)

    outputs = jnp.dot(tokens, whole, preferred_element_type=F32)
    errors = (outputs - target).astype(BF16)
    everyone = exchange(jnp.broadcast_to(errors, (PLANE, count, width)), ("x", "y"))
    inputs_grad = lax.dot_general(
        errors, whole, (((1,), (1,)), ((), ())), preferred_element_type=F32
    ).astype(BF16)

    parts = grad_parts(features, everyone, mask, scale)
    parts = exchange(parts.reshape(OWNERS, -1, width), ("c", "z"))
    selected = exchange(sum_and_copy(parts, OWNERS), ("x", "y", "c")).reshape(shard_rows, width)

    first, last = bounds[0, 0, 0], bounds[0, 0, 1]
    slots = []
    for s in range(3 * tiles // (2 * OWNERS)):
        at = jnp.minimum(first + s, tiles - 1) * TILE_ROWS
        tile = lax.dynamic_slice_in_dim(selected, at, TILE_ROWS, 0).astype(F32)
        slots.append(jnp.where(s < last - first, tile, 0.0).reshape(-1))
    return inputs_grad, selected, jnp.stack(slots)[None, None]


def solution(mesh):
    fine = Mesh(mesh.devices.reshape(NX, NY, NC, NZ), ("x", "y", "c", "z"))
    dp = ("x", "y", "c")
    return jax.shard_map(
        body,
        mesh=fine,
        in_specs=(
            P((*dp, "z"), None),
            P("z", None),
            P((*dp, "z"), None),
            P("z", dp, None),
            P(dp, "z", None),
        ),
        out_specs=(P((*dp, "z"), None), P("z", None), P("z", dp, None, None)),
        check_vma=False,
    )
```

```python
import functools
import math

import jax
import jax.numpy as jnp
from jax import lax
from jax.experimental import pallas as pl
from jax.experimental.pallas import tpu as pltpu
from jax.sharding import Mesh, PartitionSpec as P

TILE_ROWS = 8
NX, NY, NC, NZ = 4, 4, 2, 16
GROUP = NY * NC
OWNERS = NX * GROUP
F32, BF16 = jnp.float32, jnp.bfloat16
VMEM_LIMIT = 48 * 1024 * 1024


def cut_kernel(tok_ref, out_ref):
    turned = tok_ref[...].T
    shares, bands, _, part, count = out_ref.shape
    out_ref[:, :, 0] = turned.reshape(bands, shares, part, count).swapaxes(0, 1)


def cut_tokens(tokens):
    count, width = tokens.shape
    rows = width // NZ
    part = rows // OWNERS
    return pl.pallas_call(
        cut_kernel,
        grid=(NZ,),
        in_specs=[pl.BlockSpec((count, rows), lambda j: (0, j))],
        out_specs=pl.BlockSpec((GROUP, NX, 1, part, count), lambda j: (0, 0, j, 0, 0)),
        out_shape=jax.ShapeDtypeStruct((GROUP, NX, NZ, part, count), tokens.dtype),
        compiler_params=pltpu.CompilerParams(vmem_limit_bytes=VMEM_LIMIT),
        cost_estimate=pl.CostEstimate(flops=0, bytes_accessed=4 * count * width, transcendentals=0),
        name="cut_tokens",
    )(tokens)


def forward_kernel(feat_ref, packed_ref, out_ref, rows):
    shards, _, width = packed_ref.shape
    count = feat_ref.shape[2]
    part = rows.shape[2]

    @pl.when(pl.program_id(0) == 0)
    def _():
        for x in range(NX):
            rows[x] = packed_ref[:, x * part : (x + 1) * part, :]

    out_ref[0, :count] = lax.dot_general(
        feat_ref[0],
        rows[...].reshape(-1, width),
        (((0,), (0,)), ((), ())),
        preferred_element_type=F32,
    ).astype(BF16)
    hits = packed_ref[:, NX * part :, :].astype(F32)
    out_ref[0, count:] = jnp.sum(hits, axis=1).astype(BF16)


def forward_parts(features, packed):
    members, depth, count = features.shape
    shards, block, width = packed.shape
    return pl.pallas_call(
        forward_kernel,
        grid=(members,),
        in_specs=[
            pl.BlockSpec((1, depth, count), lambda i: (i, 0, 0)),
            pl.BlockSpec((shards, block, width), lambda i: (0, 0, 0)),
        ],
        out_specs=pl.BlockSpec((1, count + shards, width), lambda i: (i, 0, 0)),
        out_shape=jax.ShapeDtypeStruct((members, count + shards, width), BF16),
        scratch_shapes=[pltpu.VMEM((NX, shards, depth // (NX * shards), width), BF16)],
        compiler_params=pltpu.CompilerParams(vmem_limit_bytes=VMEM_LIMIT),
        cost_estimate=pl.CostEstimate(
            flops=2 * members * depth * count * width,
            bytes_accessed=2 * (members * count * (depth + width) + depth * width),
            transcendentals=0,
        ),
        name="forward_parts",
    )(features, packed)


def error_kernel(parts_ref, target_ref, out_ref, copies_ref):
    count = target_ref.shape[0]
    outputs = jnp.sum(parts_ref[:, :count, :].astype(F32), axis=0)
    errors = (outputs - target_ref[...].astype(F32)).astype(BF16)
    out_ref[...] = errors
    copies_ref[...] = jnp.broadcast_to(errors[None], copies_ref.shape)


def sum_errors(parts, target):
    return pl.pallas_call(
        error_kernel,
        out_shape=(
            jax.ShapeDtypeStruct(target.shape, BF16),
            jax.ShapeDtypeStruct((parts.shape[0], *target.shape), BF16),
        ),
        compiler_params=pltpu.CompilerParams(vmem_limit_bytes=VMEM_LIMIT),
        name="sum_errors",
    )(parts, target)


def mask_kernel(place_ref, feat_ref, hits_ref, out_ref):
    depth = feat_ref.shape[1]
    shards, lanes = hits_ref.shape[1:]
    part = depth // (NX * shards)
    each = part // TILE_ROWS
    row = lax.broadcasted_iota(jnp.int32, (depth, shards), 0)
    at = lax.broadcasted_iota(jnp.int32, (depth, shards), 1)
    shard = (row // part) % shards == at
    row = lax.broadcasted_iota(jnp.int32, (depth, lanes), 0)
    at = lax.broadcasted_iota(jnp.int32, (depth, lanes), 1)
    tile = (row // (part * shards) * GROUP + place_ref[0]) * each + row // TILE_ROWS % each
    hits = jnp.dot(shard.astype(BF16), hits_ref[0], preferred_element_type=F32)
    hits = jnp.where(tile == at, hits, 0.0).astype(BF16)
    keep = jnp.dot(hits, jnp.ones((lanes, out_ref.shape[1]), BF16), preferred_element_type=F32)
    out_ref[...] = feat_ref[0] * keep.astype(BF16)


def mask_features(place, features, parts):
    members, depth, count = features.shape
    lanes = 128
    return pl.pallas_call(
        mask_kernel,
        grid=(members,),
        in_specs=[
            pl.BlockSpec(memory_space=pltpu.SMEM),
            pl.BlockSpec((1, depth, count), lambda i: (i, 0, 0)),
            pl.BlockSpec((1, NZ, lanes), lambda i: (i, count // NZ, 0)),
        ],
        out_specs=pl.BlockSpec((depth, count), lambda i: (0, i)),
        out_shape=jax.ShapeDtypeStruct((depth, members * count), BF16),
        compiler_params=pltpu.CompilerParams(vmem_limit_bytes=VMEM_LIMIT),
        cost_estimate=pl.CostEstimate(
            flops=2 * members * depth * lanes * (NZ + count),
            bytes_accessed=4 * members * depth * count,
            transcendentals=0,
        ),
        name="mask_features",
    )(place, features, parts)


def grad_kernel(scale, feat_ref, err_ref, out_ref):
    out_ref[...] = (
        jnp.dot(feat_ref[...], err_ref[...], preferred_element_type=F32) * scale
    ).astype(BF16)


def grad_parts(features, errors, scale):
    depth, count = features.shape
    width = errors.shape[1]
    step = depth // NX
    return pl.pallas_call(
        functools.partial(grad_kernel, scale),
        grid=(NX,),
        in_specs=[
            pl.BlockSpec((step, count), lambda i: (i, 0)),
            pl.BlockSpec((count, width), lambda i: (0, 0)),
        ],
        out_specs=pl.BlockSpec((step, width), lambda i: (i, 0)),
        out_shape=jax.ShapeDtypeStruct((depth, width), BF16),
        compiler_params=pltpu.CompilerParams(vmem_limit_bytes=VMEM_LIMIT),
        cost_estimate=pl.CostEstimate(
            flops=2 * depth * count * width,
            bytes_accessed=2 * (count * (depth + width) + depth * width),
            transcendentals=0,
        ),
        name="grad_parts",
    )(features, errors)


def sum_kernel(parts_ref, out_ref):
    total = jnp.sum(parts_ref[...].astype(F32), axis=0).astype(BF16)
    out_ref[...] = jnp.broadcast_to(total[None], out_ref.shape)


def sum_and_copy(parts, copies):
    return pl.pallas_call(
        sum_kernel,
        out_shape=jax.ShapeDtypeStruct((copies, *parts.shape[1:]), BF16),
        compiler_params=pltpu.CompilerParams(vmem_limit_bytes=VMEM_LIMIT),
        name="sum_and_copy",
    )(parts)


def exchange(parts, axes):
    return lax.all_to_all(parts, axes, split_axis=0, concat_axis=0, tiled=True)


def body(tokens, weight, target, bounds, kept):
    count, model = tokens.shape
    shard_rows, width = weight.shape
    tiles = shard_rows // TILE_ROWS
    scale = 1.0 / math.sqrt(count * NZ * OWNERS)
    part = shard_rows // OWNERS
    group = ("y", "c")
    place = lax.axis_index(group)

    whole = lax.all_gather(weight, "z", axis=0, tiled=True)

    rows = weight.reshape(NX, GROUP, part, width)
    rows = lax.dynamic_index_in_dim(rows, place, 1, keepdims=False).reshape(NX * part, width)
    hits = jnp.any(kept.reshape(-1, 1) == jnp.arange(width, dtype=jnp.int32), axis=0)
    hits = jnp.pad(hits.astype(BF16)[None], ((0, part - 1), (0, 0)))
    cut = cut_tokens(tokens)
    packed, cut = lax.optimization_barrier((jnp.concatenate([rows, hits]), cut))
    features = exchange(cut, group).reshape(GROUP, model // GROUP, count)
    packed = lax.all_gather(packed, "z", axis=0, tiled=False)

    outputs = exchange(forward_parts(features, packed), group)
    errors, copies = sum_errors(outputs, target)
    everyone = exchange(copies, group).reshape(-1, width)
    masked = mask_features(place.reshape(1), features, outputs)

    parts = exchange(grad_parts(masked, everyone, scale).reshape(NX, -1, width), "x")
    parts = jnp.sum(parts.astype(F32), axis=0).astype(BF16).reshape(NZ, part, width)
    parts = exchange(parts, "z")

    inputs_grad = lax.dot_general(
        errors, whole, (((1,), (1,)), ((), ())), preferred_element_type=F32
    ).astype(BF16)
    parts, inputs_grad = lax.optimization_barrier((parts, inputs_grad))
    selected = exchange(sum_and_copy(parts, OWNERS), ("x", *group)).reshape(shard_rows, width)

    first, last = bounds[0, 0, 0], bounds[0, 0, 1]
    slots = []
    for s in range(3 * tiles // (2 * OWNERS)):
        at = jnp.minimum(first + s, tiles - 1) * TILE_ROWS
        tile = lax.dynamic_slice_in_dim(selected, at, TILE_ROWS, 0).astype(F32)
        slots.append(jnp.where(s < last - first, tile, 0.0).reshape(-1))
    return inputs_grad, selected, jnp.stack(slots)[None, None]


def solution(mesh):
    fine = Mesh(mesh.devices.reshape(NX, NY, NC, NZ), ("x", "y", "c", "z"))
    dp = ("x", "y", "c")
    return jax.shard_map(
        body,
        mesh=fine,
        in_specs=(
            P((*dp, "z"), None),
            P("z", None),
            P((*dp, "z"), None),
            P("z", dp, None),
            P(dp, "z", None),
        ),
        out_specs=(P((*dp, "z"), None), P("z", None), P("z", dp, None, None)),
        check_vma=False,
    )
```

```python
import functools
import math

import jax
import jax.numpy as jnp
from jax import lax
from jax.experimental import pallas as pl
from jax.experimental.pallas import tpu as pltpu
from jax.sharding import Mesh, PartitionSpec as P

TILE_ROWS = 8
NX, NY, NC, NZ = 4, 4, 2, 16
GROUP = NY * NC
OWNERS = NX * GROUP
F32, BF16 = jnp.float32, jnp.bfloat16
VMEM_MB = 1024 * 1024
LANES = 128


def params(megabytes):
    return pltpu.CompilerParams(vmem_limit_bytes=megabytes * VMEM_MB)


def cut_kernel(place_ref, tok_ref, weight_ref, kept_ref, out_ref, packed_ref):
    shares, bands, _, part, count = out_ref.shape
    turned = tok_ref[...].T
    out_ref[:, :, 0] = turned.reshape(bands, shares, part, count).swapaxes(0, 1)

    @pl.when(pl.program_id(0) == 0)
    def _():
        rows = bands * part
        blocks = weight_ref.shape[3] // LANES
        for b in range(blocks):
            block = weight_ref[:, 0, :, b * LANES : (b + 1) * LANES]
            packed_ref[b * rows : (b + 1) * rows] = block.reshape(rows, LANES)
        lane = lax.broadcasted_iota(jnp.int32, (part, LANES), 1)
        hits = jnp.zeros((part, LANES), F32)
        for k in range(kept_ref.shape[0]):
            hits = jnp.where(lane == kept_ref[k], 1.0, hits)
        first = lax.broadcasted_iota(jnp.int32, (part, LANES), 0) == 0
        packed_ref[blocks * rows :] = jnp.where(first, hits, 0.0).astype(BF16)


def cut_tokens(place, tokens, weight, kept):
    count, model = tokens.shape
    rows = model // NZ
    part = rows // OWNERS
    width = weight.shape[1]
    packed = (NX * width // LANES + 1) * part
    return pl.pallas_call(
        cut_kernel,
        grid_spec=pltpu.PrefetchScalarGridSpec(
            num_scalar_prefetch=1,
            grid=(NZ,),
            in_specs=[
                pl.BlockSpec((count, rows), lambda j, at: (0, j)),
                pl.BlockSpec((NX, 1, part, width), lambda j, at: (0, at[0], 0, 0)),
                pl.BlockSpec(memory_space=pltpu.SMEM),
            ],
            out_specs=[
                pl.BlockSpec((GROUP, NX, 1, part, count), lambda j, at: (0, 0, j, 0, 0)),
                pl.BlockSpec((packed, LANES), lambda j, at: (0, 0)),
            ],
        ),
        out_shape=[
            jax.ShapeDtypeStruct((GROUP, NX, NZ, part, count), BF16),
            jax.ShapeDtypeStruct((packed, LANES), BF16),
        ],
        compiler_params=params(60),
        cost_estimate=pl.CostEstimate(flops=0, bytes_accessed=4 * count * model, transcendentals=0),
        name="cut_tokens",
    )(place, tokens, weight.reshape(NX, GROUP, part, width), kept)


def unpack_rows(packed_ref, rows):
    bands, _, part, width = rows.shape
    for b in range(width // LANES):
        for x in range(bands):
            at = (b * bands + x) * part
            rows[x, :, :, b * LANES : (b + 1) * LANES] = packed_ref[:, at : at + part, :]


def forward_kernel(core_ref, feat_ref, packed_ref, out_ref, rows):
    width = rows.shape[3]
    count = feat_ref.shape[3]

    @pl.when(pl.program_id(0) == 0)
    def _():
        unpack_rows(packed_ref, rows)

    out_ref[0, :count] = lax.dot_general(
        feat_ref[0, 0],
        rows[...].reshape(-1, width),
        (((0,), (0,)), ((), ())),
        preferred_element_type=F32,
    ).astype(out_ref.dtype)
    if out_ref.shape[1] > count:
        out_ref[0, count:] = jnp.zeros((out_ref.shape[1] - count, width), BF16)
        out_ref[0, count:, :LANES] = read_hits(packed_ref[:, NX * rows.shape[2] * width // LANES :, :])


def read_hits(block):
    return jnp.sum(block.astype(F32), axis=1).astype(BF16)


def forward_parts(core, features, packed, kind, extra, name):
    members, _, depth, count = features.shape
    shards, block, _ = packed.shape
    part = depth // (NX * shards)
    width = (block // part - 1) // NX * LANES
    return pl.pallas_call(
        forward_kernel,
        grid_spec=pltpu.PrefetchScalarGridSpec(
            num_scalar_prefetch=1,
            grid=(members,),
            in_specs=[
                pl.BlockSpec((1, 1, depth, count), lambda i, at: (i, at[0], 0, 0)),
                pl.BlockSpec((shards, block, LANES), lambda i, at: (0, 0, 0)),
            ],
            out_specs=pl.BlockSpec((1, count + extra, width), lambda i, at: (i, 0, 0)),
            scratch_shapes=[pltpu.VMEM((NX, shards, part, width), BF16)],
        ),
        out_shape=jax.ShapeDtypeStruct((members, count + extra, width), kind),
        compiler_params=params(40),
        cost_estimate=pl.CostEstimate(
            flops=2 * members * depth * count * width,
            bytes_accessed=2 * (members * count * (depth + width) + depth * width),
            transcendentals=0,
        ),
        name=name,
    )(core, features, packed)


def join_kernel(core_ref, own_ref, got_ref, packed_ref, out_ref):
    count = own_ref.shape[1]
    shards = packed_ref.shape[0]
    out_ref[:, :count] = (own_ref[...] + got_ref[:, :count, :].astype(F32)).astype(BF16)
    mine = read_hits(packed_ref[...]).astype(F32)
    other = got_ref[0, count:, :LANES].astype(F32)
    members, _, width = got_ref.shape
    for c in range(NC):
        at = slice(count + c * shards, count + (c + 1) * shards)
        hits = jnp.where(core_ref[0] == c, mine, other).astype(BF16)
        out_ref[:, at] = jnp.zeros((members, shards, width), BF16)
        out_ref[:, at, :LANES] = jnp.broadcast_to(hits[None], (members, shards, LANES))


def join_parts(core, own, got, packed):
    members, count, width = own.shape
    shards, block, _ = packed.shape
    part = got.shape[1] - count
    return pl.pallas_call(
        join_kernel,
        grid=(1,),
        in_specs=[
            pl.BlockSpec(memory_space=pltpu.SMEM),
            pl.BlockSpec(own.shape, lambda i: (0, 0, 0)),
            pl.BlockSpec(got.shape, lambda i: (0, 0, 0)),
            pl.BlockSpec((shards, part, LANES), lambda i: (0, block // part - 1, 0)),
        ],
        out_specs=pl.BlockSpec((members, count + NC * shards, width), lambda i: (0, 0, 0)),
        out_shape=jax.ShapeDtypeStruct((members, count + NC * shards, width), BF16),
        compiler_params=params(40),
        name="join_parts",
    )(core, own, got, packed)


def error_kernel(parts_ref, target_ref, out_ref, copies_ref):
    count = target_ref.shape[0]
    outputs = jnp.sum(parts_ref[:, :count, :].astype(F32), axis=0)
    errors = (outputs - target_ref[...].astype(F32)).astype(BF16)
    out_ref[...] = errors
    copies_ref[...] = jnp.broadcast_to(errors[None], copies_ref.shape)


def sum_errors(parts, target):
    return pl.pallas_call(
        error_kernel,
        out_shape=(
            jax.ShapeDtypeStruct(target.shape, BF16),
            jax.ShapeDtypeStruct((parts.shape[0], *target.shape), BF16),
        ),
        compiler_params=params(40),
        name="sum_errors",
    )(parts, target)


def mask_kernel(place_ref, feat_ref, hits_ref, out_ref):
    depth = feat_ref.shape[1]
    shards, lanes = hits_ref.shape[1:]
    part = depth // (NX * shards)
    each = part // TILE_ROWS
    row = lax.broadcasted_iota(jnp.int32, (depth, shards), 0)
    at = lax.broadcasted_iota(jnp.int32, (depth, shards), 1)
    shard = (row // part) % shards == at
    row = lax.broadcasted_iota(jnp.int32, (depth, lanes), 0)
    at = lax.broadcasted_iota(jnp.int32, (depth, lanes), 1)
    tile = (row // (part * shards) * GROUP + place_ref[0]) * each + row // TILE_ROWS % each
    hits = jnp.dot(shard.astype(BF16), hits_ref[0], preferred_element_type=F32)
    hits = jnp.where(tile == at, hits, 0.0).astype(BF16)
    keep = jnp.dot(hits, jnp.ones((lanes, out_ref.shape[1]), BF16), preferred_element_type=F32)
    out_ref[...] = feat_ref[0] * keep.astype(BF16)


def mask_features(place, features, parts):
    members, depth, count = features.shape
    return pl.pallas_call(
        mask_kernel,
        grid_spec=pltpu.PrefetchScalarGridSpec(
            num_scalar_prefetch=1,
            grid=(members,),
            in_specs=[
                pl.BlockSpec((1, depth, count), lambda i, at: (i, 0, 0)),
                pl.BlockSpec((1, NZ, LANES), lambda i, at: (i // NC, count // NZ + i % NC, 0)),
            ],
            out_specs=pl.BlockSpec((depth, count), lambda i, at: (0, i // NC + NY * ((i + at[0]) % NC))),
        ),
        out_shape=jax.ShapeDtypeStruct((depth, members * count), BF16),
        compiler_params=params(60),
        cost_estimate=pl.CostEstimate(
            flops=2 * members * depth * LANES * (NZ + count),
            bytes_accessed=4 * members * depth * count,
            transcendentals=0,
        ),
        name="mask_features",
    )(place, features, parts)


def grad_kernel(scale, feat_ref, own_ref, other_ref, out_ref):
    count = own_ref.shape[0]
    total = jnp.dot(feat_ref[:, :count], own_ref[...], preferred_element_type=F32)
    total += jnp.dot(feat_ref[:, count:], other_ref[...], preferred_element_type=F32)
    out_ref[...] = (total * scale).astype(BF16)


def grad_parts(features, own, other, scale):
    depth, both = features.shape
    count, width = own.shape
    step = depth // NX
    return pl.pallas_call(
        functools.partial(grad_kernel, scale),
        grid=(NX,),
        in_specs=[
            pl.BlockSpec((step, both), lambda i: (i, 0)),
            pl.BlockSpec((count, width), lambda i: (0, 0)),
            pl.BlockSpec((count, width), lambda i: (0, 0)),
        ],
        out_specs=pl.BlockSpec((step, width), lambda i: (i, 0)),
        out_shape=jax.ShapeDtypeStruct((depth, width), BF16),
        compiler_params=params(60),
        cost_estimate=pl.CostEstimate(
            flops=2 * depth * both * width,
            bytes_accessed=2 * (both * (depth + width) + depth * width),
            transcendentals=0,
        ),
        name="grad_parts",
    )(features, own, other)


def sum_kernel(parts_ref, out_ref):
    total = jnp.sum(parts_ref[...].astype(F32), axis=0).astype(BF16)
    out_ref[...] = jnp.broadcast_to(total[None], out_ref.shape)


def sum_and_copy(parts, copies):
    return pl.pallas_call(
        sum_kernel,
        out_shape=jax.ShapeDtypeStruct((copies, *parts.shape[1:]), BF16),
        compiler_params=params(40),
        name="sum_and_copy",
    )(parts)


def exchange(parts, axes):
    return lax.all_to_all(parts, axes, split_axis=0, concat_axis=0, tiled=True)


def body(tokens, weight, target, bounds, kept):
    count, model = tokens.shape
    shard_rows, width = weight.shape
    tiles = shard_rows // TILE_ROWS
    scale = 1.0 / math.sqrt(count * NZ * OWNERS)
    part = shard_rows // OWNERS
    group = ("y", "c")
    place = lax.axis_index(group).reshape(1)
    core = lax.axis_index("c").reshape(1)
    swap = [(0, 1), (1, 0)]

    whole = lax.all_gather(weight, "z", axis=0, tiled=True)

    cut, packed = cut_tokens(place, tokens, weight, kept.reshape(-1))
    features = exchange(cut, group).reshape(NY, NC, model // GROUP, count)
    packed = lax.all_gather(packed, "z", axis=0, tiled=False)

    other = forward_parts(1 - core, features, packed, BF16, NZ, "forward_other")
    got = lax.ppermute(other, "c", swap)
    own = forward_parts(core, features, packed, F32, 0, "forward_own")
    outputs = exchange(join_parts(core, own, got, packed), "y")
    errors, copies = sum_errors(outputs, target)
    own = exchange(copies, "y").reshape(-1, width)
    masked = mask_features(place, features.reshape(GROUP, -1, count), outputs)
    own, masked = lax.optimization_barrier((own, masked))
    other = lax.ppermute(own, "c", swap)

    parts = exchange(grad_parts(masked, own, other, scale).reshape(NX, -1, width), "x")
    parts = jnp.sum(parts.astype(F32), axis=0).astype(BF16).reshape(NZ, part, width)
    parts = exchange(parts, "z")

    inputs_grad = lax.dot_general(
        errors, whole, (((1,), (1,)), ((), ())), preferred_element_type=F32
    ).astype(BF16)
    parts, inputs_grad = lax.optimization_barrier((parts, inputs_grad))
    selected = exchange(sum_and_copy(parts, OWNERS), ("x", *group)).reshape(shard_rows, width)

    first, last = bounds[0, 0, 0], bounds[0, 0, 1]
    slots = []
    for s in range(3 * tiles // (2 * OWNERS)):
        at = jnp.minimum(first + s, tiles - 1) * TILE_ROWS
        tile = lax.dynamic_slice_in_dim(selected, at, TILE_ROWS, 0).astype(F32)
        slots.append(jnp.where(s < last - first, tile, 0.0).reshape(-1))
    return inputs_grad, selected, jnp.stack(slots)[None, None]


def solution(mesh):
    fine = Mesh(mesh.devices.reshape(NX, NY, NC, NZ), ("x", "y", "c", "z"))
    dp = ("x", "y", "c")
    return jax.shard_map(
        body,
        mesh=fine,
        in_specs=(
            P((*dp, "z"), None),
            P("z", None),
            P((*dp, "z"), None),
            P("z", dp, None),
            P(dp, "z", None),
        ),
        out_specs=(P((*dp, "z"), None), P("z", None), P("z", dp, None, None)),
        check_vma=False,
    )
```

```python
import functools
import math

import jax
import jax.numpy as jnp
from jax import lax
from jax.experimental import pallas as pl
from jax.experimental.pallas import tpu as pltpu
from jax.sharding import Mesh, PartitionSpec as P

TILE_ROWS = 8
NX, NY, NC, NZ = 4, 4, 2, 16
GROUP = NY * NC
OWNERS = NX * GROUP
F32, BF16 = jnp.float32, jnp.bfloat16
VMEM_MB = 1024 * 1024
LANES = 128


def params(megabytes):
    return pltpu.CompilerParams(vmem_limit_bytes=megabytes * VMEM_MB)


def cut_kernel(place_ref, tok_ref, weight_ref, kept_ref, out_ref, packed_ref):
    shares, bands, shards, part, count = out_ref.shape
    rows = bands * shares * part
    for j in range(shards):
        turned = tok_ref[:, j * rows : (j + 1) * rows].T
        out_ref[:, :, j] = turned.reshape(bands, shares, part, count).swapaxes(0, 1)

    @pl.when(pl.program_id(0) == 0)
    def _():
        rows = bands * part
        blocks = weight_ref.shape[3] // LANES
        for b in range(blocks):
            block = weight_ref[:, 0, :, b * LANES : (b + 1) * LANES]
            packed_ref[b * rows : (b + 1) * rows] = block.reshape(rows, LANES)
        lane = lax.broadcasted_iota(jnp.int32, (part, LANES), 1)
        hits = jnp.zeros((part, LANES), F32)
        for k in range(kept_ref.shape[0]):
            hits = jnp.where(lane == kept_ref[k], 1.0, hits)
        first = lax.broadcasted_iota(jnp.int32, (part, LANES), 0) == 0
        packed_ref[blocks * rows :] = jnp.where(first, hits, 0.0).astype(BF16)


def cut_tokens(place, tokens, weight, kept):
    count, model = tokens.shape
    rows = model // NZ
    part = rows // OWNERS
    width = weight.shape[1]
    packed = (NX * width // LANES + 1) * part
    step = NZ // 2
    return pl.pallas_call(
        cut_kernel,
        grid_spec=pltpu.PrefetchScalarGridSpec(
            num_scalar_prefetch=1,
            grid=(NZ // step,),
            in_specs=[
                pl.BlockSpec((count, rows * step), lambda j, at: (0, j)),
                pl.BlockSpec((NX, 1, part, width), lambda j, at: (0, at[0], 0, 0)),
                pl.BlockSpec(memory_space=pltpu.SMEM),
            ],
            out_specs=[
                pl.BlockSpec((GROUP, NX, step, part, count), lambda j, at: (0, 0, j, 0, 0)),
                pl.BlockSpec((packed, LANES), lambda j, at: (0, 0)),
            ],
        ),
        out_shape=[
            jax.ShapeDtypeStruct((GROUP, NX, NZ, part, count), BF16),
            jax.ShapeDtypeStruct((packed, LANES), BF16),
        ],
        compiler_params=params(60),
        cost_estimate=pl.CostEstimate(flops=0, bytes_accessed=4 * count * model, transcendentals=0),
        name="cut_tokens",
    )(place, tokens, weight.reshape(NX, GROUP, part, width), kept)


def unpack_rows(packed_ref, rows):
    bands, _, part, width = rows.shape
    for b in range(width // LANES):
        for x in range(bands):
            at = (b * bands + x) * part
            rows[x, :, :, b * LANES : (b + 1) * LANES] = packed_ref[:, at : at + part, :]


def forward_kernel(core_ref, feat_ref, packed_ref, out_ref, rows):
    width = rows.shape[3]
    count = feat_ref.shape[3]

    @pl.when(pl.program_id(0) == 0)
    def _():
        unpack_rows(packed_ref, rows)

    out_ref[0, :count] = lax.dot_general(
        feat_ref[0, 0],
        rows[...].reshape(-1, width),
        (((0,), (0,)), ((), ())),
        preferred_element_type=F32,
    ).astype(out_ref.dtype)
    if out_ref.shape[1] > count:
        out_ref[0, count:] = jnp.zeros((out_ref.shape[1] - count, width), BF16)
        out_ref[0, count:, :LANES] = read_hits(packed_ref[:, NX * rows.shape[2] * width // LANES :, :])


def read_hits(block):
    return jnp.sum(block.astype(F32), axis=1).astype(BF16)


def forward_parts(core, features, packed, kind, extra, name):
    members, _, depth, count = features.shape
    shards, block, _ = packed.shape
    part = depth // (NX * shards)
    width = (block // part - 1) // NX * LANES
    return pl.pallas_call(
        forward_kernel,
        grid_spec=pltpu.PrefetchScalarGridSpec(
            num_scalar_prefetch=1,
            grid=(members,),
            in_specs=[
                pl.BlockSpec((1, 1, depth, count), lambda i, at: (i, at[0], 0, 0)),
                pl.BlockSpec((shards, block, LANES), lambda i, at: (0, 0, 0)),
            ],
            out_specs=pl.BlockSpec((1, count + extra, width), lambda i, at: (i, 0, 0)),
            scratch_shapes=[pltpu.VMEM((NX, shards, part, width), BF16)],
        ),
        out_shape=jax.ShapeDtypeStruct((members, count + extra, width), kind),
        compiler_params=params(40),
        cost_estimate=pl.CostEstimate(
            flops=2 * members * depth * count * width,
            bytes_accessed=2 * (members * count * (depth + width) + depth * width),
            transcendentals=0,
        ),
        name=name,
    )(core, features, packed)


def join_kernel(core_ref, own_ref, got_ref, packed_ref, out_ref):
    count = own_ref.shape[1]
    shards = packed_ref.shape[0]
    out_ref[:, :count] = (own_ref[...] + got_ref[:, :count, :].astype(F32)).astype(BF16)
    mine = read_hits(packed_ref[...]).astype(F32)
    other = got_ref[0, count:, :LANES].astype(F32)
    members, _, width = got_ref.shape
    for c in range(NC):
        at = slice(count + c * shards, count + (c + 1) * shards)
        hits = jnp.where(core_ref[0] == c, mine, other).astype(BF16)
        out_ref[:, at] = jnp.zeros((members, shards, width), BF16)
        out_ref[:, at, :LANES] = jnp.broadcast_to(hits[None], (members, shards, LANES))


def join_parts(core, own, got, packed):
    members, count, width = own.shape
    shards, block, _ = packed.shape
    part = got.shape[1] - count
    return pl.pallas_call(
        join_kernel,
        grid=(1,),
        in_specs=[
            pl.BlockSpec(memory_space=pltpu.SMEM),
            pl.BlockSpec(own.shape, lambda i: (0, 0, 0)),
            pl.BlockSpec(got.shape, lambda i: (0, 0, 0)),
            pl.BlockSpec((shards, part, LANES), lambda i: (0, block // part - 1, 0)),
        ],
        out_specs=pl.BlockSpec((members, count + NC * shards, width), lambda i: (0, 0, 0)),
        out_shape=jax.ShapeDtypeStruct((members, count + NC * shards, width), BF16),
        compiler_params=params(40),
        name="join_parts",
    )(core, own, got, packed)


def error_kernel(parts_ref, target_ref, out_ref, copies_ref):
    count = target_ref.shape[0]
    outputs = jnp.sum(parts_ref[:, :count, :].astype(F32), axis=0)
    errors = (outputs - target_ref[...].astype(F32)).astype(BF16)
    out_ref[...] = errors
    copies_ref[...] = jnp.broadcast_to(errors[None], copies_ref.shape)


def sum_errors(parts, target):
    return pl.pallas_call(
        error_kernel,
        out_shape=(
            jax.ShapeDtypeStruct(target.shape, BF16),
            jax.ShapeDtypeStruct((parts.shape[0], *target.shape), BF16),
        ),
        compiler_params=params(40),
        name="sum_errors",
    )(parts, target)


def mask_kernel(place_ref, feat_ref, hits_ref, out_ref):
    members, _, depth, count = feat_ref.shape
    shards, lanes = hits_ref.shape[1:]
    part = depth // (NX * shards)
    each = part // TILE_ROWS
    row = lax.broadcasted_iota(jnp.int32, (depth, shards), 0)
    at = lax.broadcasted_iota(jnp.int32, (depth, shards), 1)
    shard = ((row // part) % shards == at).astype(BF16)
    row = lax.broadcasted_iota(jnp.int32, (depth, lanes), 0)
    at = lax.broadcasted_iota(jnp.int32, (depth, lanes), 1)
    tile = (row // (part * shards) * GROUP + place_ref[0]) * each + row // TILE_ROWS % each
    ones = jnp.ones((lanes, count), BF16)
    for y in range(members):
        hits = jnp.dot(shard, hits_ref[y], preferred_element_type=F32)
        hits = jnp.where(tile == at, hits, 0.0).astype(BF16)
        keep = jnp.dot(hits, ones, preferred_element_type=F32)
        out_ref[0, y] = feat_ref[y, 0] * keep.astype(BF16)


def mask_features(place, features, parts):
    members, cores, depth, count = features.shape
    return pl.pallas_call(
        mask_kernel,
        grid_spec=pltpu.PrefetchScalarGridSpec(
            num_scalar_prefetch=1,
            grid=(cores,),
            in_specs=[
                pl.BlockSpec((members, 1, depth, count), lambda o, at: (0, (o + at[0]) % NC, 0, 0)),
                pl.BlockSpec((members, NZ, LANES), lambda o, at: (0, count // NZ + (o + at[0]) % NC, 0)),
            ],
            out_specs=pl.BlockSpec((1, members, depth, count), lambda o, at: (o, 0, 0, 0)),
        ),
        out_shape=jax.ShapeDtypeStruct((cores, members, depth, count), BF16),
        compiler_params=params(60),
        cost_estimate=pl.CostEstimate(
            flops=2 * cores * members * depth * LANES * (NZ + count),
            bytes_accessed=4 * cores * members * depth * count,
            transcendentals=0,
        ),
        name="mask_features",
    )(place, features, parts)


def grad_kernel(scale, feat_ref, own_ref, other_ref, out_ref):
    total = 0.0
    for o, errors in enumerate((own_ref, other_ref)):
        features = jnp.concatenate([feat_ref[o, y] for y in range(feat_ref.shape[1])], axis=1)
        total += jnp.dot(features, errors[...], preferred_element_type=F32)
    out_ref[...] = (total * scale).astype(BF16)


def grad_parts(features, own, other, scale):
    cores, members, depth, count = features.shape
    both, width = own.shape
    step = depth // 2
    return pl.pallas_call(
        functools.partial(grad_kernel, scale),
        grid=(depth // step,),
        in_specs=[
            pl.BlockSpec((cores, members, step, count), lambda i: (0, 0, i, 0)),
            pl.BlockSpec((both, width), lambda i: (0, 0)),
            pl.BlockSpec((both, width), lambda i: (0, 0)),
        ],
        out_specs=pl.BlockSpec((step, width), lambda i: (i, 0)),
        out_shape=jax.ShapeDtypeStruct((depth, width), BF16),
        compiler_params=params(56),
        cost_estimate=pl.CostEstimate(
            flops=2 * depth * cores * both * width,
            bytes_accessed=2 * (cores * both * (depth + width) + depth * width),
            transcendentals=0,
        ),
        name="grad_parts",
    )(features, own, other)


def sum_kernel(parts_ref, out_ref):
    total = jnp.sum(parts_ref[...].astype(F32), axis=0).astype(BF16)
    out_ref[...] = jnp.broadcast_to(total[None], out_ref.shape)


def sum_and_copy(parts, copies):
    return pl.pallas_call(
        sum_kernel,
        out_shape=jax.ShapeDtypeStruct((copies, *parts.shape[1:]), BF16),
        compiler_params=params(40),
        name="sum_and_copy",
    )(parts)


def exchange(parts, axes):
    return lax.all_to_all(parts, axes, split_axis=0, concat_axis=0, tiled=True)


def body(tokens, weight, target, bounds, kept):
    count, model = tokens.shape
    shard_rows, width = weight.shape
    tiles = shard_rows // TILE_ROWS
    scale = 1.0 / math.sqrt(count * NZ * OWNERS)
    part = shard_rows // OWNERS
    group = ("y", "c")
    place = lax.axis_index(group).reshape(1)
    core = lax.axis_index("c").reshape(1)
    swap = [(0, 1), (1, 0)]

    cut, packed = cut_tokens(place, tokens, weight, kept.reshape(-1))
    features = exchange(cut, group).reshape(NY, NC, model // GROUP, count)
    packed = lax.all_gather(packed, "z", axis=0, tiled=False)
    weight, packed, features = lax.optimization_barrier((weight, packed, features))
    whole = lax.all_gather(weight, "z", axis=0, tiled=True)

    other = forward_parts(1 - core, features, packed, BF16, NZ, "forward_other")
    got = lax.ppermute(other, "c", swap)
    own = forward_parts(core, features, packed, F32, 0, "forward_own")
    outputs = exchange(join_parts(core, own, got, packed), "y")
    errors, copies = sum_errors(outputs, target)
    own = exchange(copies, "y").reshape(-1, width)
    masked = mask_features(place, features, outputs)
    own, masked = lax.optimization_barrier((own, masked))
    other = lax.ppermute(own, "c", swap)

    parts = exchange(grad_parts(masked, own, other, scale).reshape(NX, -1, width), "x")
    parts = jnp.sum(parts.astype(F32), axis=0).astype(BF16).reshape(NZ, part, width)
    parts = exchange(parts, "z")

    selected = exchange(sum_and_copy(parts, OWNERS), ("x", *group)).reshape(shard_rows, width)
    inputs_grad = lax.dot_general(
        errors, whole, (((1,), (1,)), ((), ())), preferred_element_type=F32
    ).astype(BF16)
    selected, inputs_grad = lax.optimization_barrier((selected, inputs_grad))

    first, last = bounds[0, 0, 0], bounds[0, 0, 1]
    slots = []
    for s in range(3 * tiles // (2 * OWNERS)):
        at = jnp.minimum(first + s, tiles - 1) * TILE_ROWS
        tile = lax.dynamic_slice_in_dim(selected, at, TILE_ROWS, 0).astype(F32)
        slots.append(jnp.where(s < last - first, tile, 0.0).reshape(-1))
    return inputs_grad, selected, jnp.stack(slots)[None, None]


def solution(mesh):
    fine = Mesh(mesh.devices.reshape(NX, NY, NC, NZ), ("x", "y", "c", "z"))
    dp = ("x", "y", "c")
    return jax.shard_map(
        body,
        mesh=fine,
        in_specs=(
            P((*dp, "z"), None),
            P("z", None),
            P((*dp, "z"), None),
            P("z", dp, None),
            P(dp, "z", None),
        ),
        out_specs=(P((*dp, "z"), None), P("z", None), P("z", dp, None, None)),
        check_vma=False,
    )
```

```python
import functools
import math

import jax
import jax.numpy as jnp
from jax import lax
from jax.experimental import pallas as pl
from jax.experimental.pallas import tpu as pltpu
from jax.sharding import Mesh, PartitionSpec as P

TILE_ROWS = 8
NX, NY, NC, NH, NL = 4, 4, 2, 4, 4
NZ = NH * NL
GROUP = NY * NC
OWNERS = NX * GROUP
F32, BF16 = jnp.float32, jnp.bfloat16
VMEM_MB = 1024 * 1024
LANES = 128


def params(megabytes):
    return pltpu.CompilerParams(vmem_limit_bytes=megabytes * VMEM_MB)


def cut_kernel(place_ref, tok_ref, weight_ref, kept_ref, out_ref, packed_ref):
    shares, bands, shards, part, count = out_ref.shape
    rows = bands * shares * part
    for j in range(shards):
        turned = tok_ref[:, j * rows : (j + 1) * rows].T
        out_ref[:, :, j] = turned.reshape(bands, shares, part, count).swapaxes(0, 1)

    @pl.when(pl.program_id(0) == 0)
    def _():
        rows = bands * part
        blocks = weight_ref.shape[3] // LANES
        for b in range(blocks):
            block = weight_ref[:, 0, :, b * LANES : (b + 1) * LANES]
            packed_ref[b * rows : (b + 1) * rows] = block.reshape(rows, LANES)
        lane = lax.broadcasted_iota(jnp.int32, (part, LANES), 1)
        hits = jnp.zeros((part, LANES), F32)
        for k in range(kept_ref.shape[0]):
            hits = jnp.where(lane == kept_ref[k], 1.0, hits)
        first = lax.broadcasted_iota(jnp.int32, (part, LANES), 0) == 0
        packed_ref[blocks * rows :] = jnp.where(first, hits, 0.0).astype(BF16)


def cut_tokens(place, tokens, weight, kept):
    count, model = tokens.shape
    rows = model // NZ
    part = rows // OWNERS
    width = weight.shape[1]
    packed = (NX * width // LANES + 1) * part
    step = NZ // 2
    return pl.pallas_call(
        cut_kernel,
        grid_spec=pltpu.PrefetchScalarGridSpec(
            num_scalar_prefetch=1,
            grid=(NZ // step,),
            in_specs=[
                pl.BlockSpec((count, rows * step), lambda j, at: (0, j)),
                pl.BlockSpec((NX, 1, part, width), lambda j, at: (0, at[0], 0, 0)),
                pl.BlockSpec(memory_space=pltpu.SMEM),
            ],
            out_specs=[
                pl.BlockSpec((GROUP, NX, step, part, count), lambda j, at: (0, 0, j, 0, 0)),
                pl.BlockSpec((packed, LANES), lambda j, at: (0, 0)),
            ],
        ),
        out_shape=[
            jax.ShapeDtypeStruct((GROUP, NX, NZ, part, count), BF16),
            jax.ShapeDtypeStruct((packed, LANES), BF16),
        ],
        compiler_params=params(60),
        cost_estimate=pl.CostEstimate(flops=0, bytes_accessed=4 * count * model, transcendentals=0),
        name="cut_tokens",
    )(place, tokens, weight.reshape(NX, GROUP, part, width), kept)


def unpack_rows(packed_ref, rows):
    bands, _, part, width = rows.shape
    for b in range(width // LANES):
        for x in range(bands):
            at = (b * bands + x) * part
            rows[x, :, :, b * LANES : (b + 1) * LANES] = packed_ref[:, at : at + part, :]


def forward_kernel(core_ref, feat_ref, packed_ref, out_ref, rows):
    width = rows.shape[3]
    count = feat_ref.shape[3]

    @pl.when(pl.program_id(0) == 0)
    def _():
        unpack_rows(packed_ref, rows)

    out_ref[0, :count] = lax.dot_general(
        feat_ref[0, 0],
        rows[...].reshape(-1, width),
        (((0,), (0,)), ((), ())),
        preferred_element_type=F32,
    ).astype(out_ref.dtype)
    if out_ref.shape[1] > count:
        out_ref[0, count:] = jnp.zeros((out_ref.shape[1] - count, width), BF16)
        out_ref[0, count:, :LANES] = read_hits(packed_ref[:, NX * rows.shape[2] * width // LANES :, :])


def read_hits(block):
    return jnp.sum(block.astype(F32), axis=1).astype(BF16)


def forward_parts(core, features, packed, kind, extra, name):
    members, _, depth, count = features.shape
    shards, block, _ = packed.shape
    part = depth // (NX * shards)
    width = (block // part - 1) // NX * LANES
    return pl.pallas_call(
        forward_kernel,
        grid_spec=pltpu.PrefetchScalarGridSpec(
            num_scalar_prefetch=1,
            grid=(members,),
            in_specs=[
                pl.BlockSpec((1, 1, depth, count), lambda i, at: (i, at[0], 0, 0)),
                pl.BlockSpec((shards, block, LANES), lambda i, at: (0, 0, 0)),
            ],
            out_specs=pl.BlockSpec((1, count + extra, width), lambda i, at: (i, 0, 0)),
            scratch_shapes=[pltpu.VMEM((NX, shards, part, width), BF16)],
        ),
        out_shape=jax.ShapeDtypeStruct((members, count + extra, width), kind),
        compiler_params=params(40),
        cost_estimate=pl.CostEstimate(
            flops=2 * members * depth * count * width,
            bytes_accessed=2 * (members * count * (depth + width) + depth * width),
            transcendentals=0,
        ),
        name=name,
    )(core, features, packed)


def join_kernel(core_ref, own_ref, got_ref, packed_ref, out_ref):
    count = own_ref.shape[1]
    shards = packed_ref.shape[0]
    out_ref[:, :count] = (own_ref[...] + got_ref[:, :count, :].astype(F32)).astype(BF16)
    mine = read_hits(packed_ref[...]).astype(F32)
    other = got_ref[0, count:, :LANES].astype(F32)
    members, _, width = got_ref.shape
    for c in range(NC):
        at = slice(count + c * shards, count + (c + 1) * shards)
        hits = jnp.where(core_ref[0] == c, mine, other).astype(BF16)
        out_ref[:, at] = jnp.zeros((members, shards, width), BF16)
        out_ref[:, at, :LANES] = jnp.broadcast_to(hits[None], (members, shards, LANES))


def join_parts(core, own, got, packed):
    members, count, width = own.shape
    shards, block, _ = packed.shape
    part = got.shape[1] - count
    return pl.pallas_call(
        join_kernel,
        grid=(1,),
        in_specs=[
            pl.BlockSpec(memory_space=pltpu.SMEM),
            pl.BlockSpec(own.shape, lambda i: (0, 0, 0)),
            pl.BlockSpec(got.shape, lambda i: (0, 0, 0)),
            pl.BlockSpec((shards, part, LANES), lambda i: (0, block // part - 1, 0)),
        ],
        out_specs=pl.BlockSpec((members, count + NC * shards, width), lambda i: (0, 0, 0)),
        out_shape=jax.ShapeDtypeStruct((members, count + NC * shards, width), BF16),
        compiler_params=params(40),
        name="join_parts",
    )(core, own, got, packed)


def error_kernel(parts_ref, target_ref, copies_ref):
    count = target_ref.shape[0]
    outputs = jnp.sum(parts_ref[:, :count, :].astype(F32), axis=0)
    errors = (outputs - target_ref[...].astype(F32)).astype(BF16)
    copies_ref[...] = jnp.broadcast_to(errors[None], copies_ref.shape)


def sum_errors(parts, target):
    return pl.pallas_call(
        error_kernel,
        out_shape=jax.ShapeDtypeStruct((parts.shape[0], *target.shape), BF16),
        compiler_params=params(40),
        name="sum_errors",
    )(parts, target)


def mask_kernel(place_ref, feat_ref, hits_ref, out_ref):
    members, _, depth, count = feat_ref.shape
    shards, lanes = hits_ref.shape[1:]
    part = depth // (NX * shards)
    each = part // TILE_ROWS
    row = lax.broadcasted_iota(jnp.int32, (depth, shards), 0)
    at = lax.broadcasted_iota(jnp.int32, (depth, shards), 1)
    shard = ((row // part) % shards == at).astype(BF16)
    row = lax.broadcasted_iota(jnp.int32, (depth, lanes), 0)
    at = lax.broadcasted_iota(jnp.int32, (depth, lanes), 1)
    tile = (row // (part * shards) * GROUP + place_ref[0]) * each + row // TILE_ROWS % each
    ones = jnp.ones((lanes, count), BF16)
    for y in range(members):
        hits = jnp.dot(shard, hits_ref[y], preferred_element_type=F32)
        hits = jnp.where(tile == at, hits, 0.0).astype(BF16)
        keep = jnp.dot(hits, ones, preferred_element_type=F32)
        out_ref[0, y] = feat_ref[y, 0] * keep.astype(BF16)


def mask_features(place, features, parts):
    members, cores, depth, count = features.shape
    return pl.pallas_call(
        mask_kernel,
        grid_spec=pltpu.PrefetchScalarGridSpec(
            num_scalar_prefetch=1,
            grid=(cores,),
            in_specs=[
                pl.BlockSpec((members, 1, depth, count), lambda o, at: (0, (o + at[0]) % NC, 0, 0)),
                pl.BlockSpec((members, NZ, LANES), lambda o, at: (0, count // NZ + (o + at[0]) % NC, 0)),
            ],
            out_specs=pl.BlockSpec((1, members, depth, count), lambda o, at: (o, 0, 0, 0)),
        ),
        out_shape=jax.ShapeDtypeStruct((cores, members, depth, count), BF16),
        compiler_params=params(60),
        cost_estimate=pl.CostEstimate(
            flops=2 * cores * members * depth * LANES * (NZ + count),
            bytes_accessed=4 * cores * members * depth * count,
            transcendentals=0,
        ),
        name="mask_features",
    )(place, features, parts)


def grad_kernel(scale, feat_ref, own_ref, other_ref, out_ref):
    total = 0.0
    for o, errors in enumerate((own_ref, other_ref)):
        features = jnp.concatenate([feat_ref[o, y] for y in range(feat_ref.shape[1])], axis=1)
        total += jnp.dot(features, errors[...], preferred_element_type=F32)
    out_ref[...] = (total * scale).astype(BF16)


def grad_parts(features, own, other, scale):
    cores, members, depth, count = features.shape
    both, width = own.shape
    step = depth // 2
    return pl.pallas_call(
        functools.partial(grad_kernel, scale),
        grid=(depth // step,),
        in_specs=[
            pl.BlockSpec((cores, members, step, count), lambda i: (0, 0, i, 0)),
            pl.BlockSpec((both, width), lambda i: (0, 0)),
            pl.BlockSpec((both, width), lambda i: (0, 0)),
        ],
        out_specs=pl.BlockSpec((step, width), lambda i: (i, 0)),
        out_shape=jax.ShapeDtypeStruct((depth, width), BF16),
        compiler_params=params(60),
        cost_estimate=pl.CostEstimate(
            flops=2 * depth * cores * both * width,
            bytes_accessed=2 * (cores * both * (depth + width) + depth * width),
            transcendentals=0,
        ),
        name="grad_parts",
    )(features, own, other)


def back_tile(y_ref, d, err_ref, rows):
    count = err_ref.shape[0] // NY
    at = pl.multiple_of((y_ref[0] + d) % NY * count, count)
    return lax.dot_general(
        rows[...].reshape(-1, rows.shape[3]),
        err_ref[pl.ds(at, count), :],
        (((1,), (1,)), ((), ())),
        preferred_element_type=F32,
    ).astype(BF16)


def back_kernel(y_ref, err_ref, packed_ref, out_ref, rows):
    unpack_rows(packed_ref, rows)
    for d in range(NY):
        out_ref[d] = back_tile(y_ref, d, err_ref, rows)


def back_join_kernel(y_ref, err_ref, packed_ref, got_ref, *outs_and_rows):
    outs, rows = outs_and_rows[:-1], outs_and_rows[-1]
    unpack_rows(packed_ref, rows)
    for d in range(NY):
        outs[d][0] = back_tile(y_ref, d, err_ref, rows)
        outs[d][1] = got_ref[d]


def back_parts(y, errors, packed, got=None):
    shards, block, _ = packed.shape
    both, width = errors.shape
    part = block // (NX * width // LANES + 1)
    depth, count = NX * shards * part, both // NY
    args = [y, errors, packed] + ([] if got is None else [got])
    if got is None:
        kernel, out_shape = back_kernel, jax.ShapeDtypeStruct((NY, depth, count), BF16)
    else:
        kernel, out_shape = back_join_kernel, [jax.ShapeDtypeStruct((NC, depth, count), BF16)] * NY
    return pl.pallas_call(
        kernel,
        in_specs=[pl.BlockSpec(memory_space=pltpu.SMEM)] + [pl.BlockSpec(memory_space=pltpu.VMEM)] * (len(args) - 1),
        out_shape=out_shape,
        scratch_shapes=[pltpu.VMEM((NX, shards, part, width), BF16)],
        compiler_params=params(40),
        cost_estimate=pl.CostEstimate(
            flops=2 * depth * both * width,
            bytes_accessed=2 * len(args) * depth * both,
            transcendentals=0,
        ),
        name="back_other" if got is None else "back_own",
    )(*args)


def place_kernel(place_ref, *refs):
    parts, out_ref, turned = refs[:NY], refs[NY], refs[NY + 1]
    y, c = place_ref[0] // NC, place_ref[0] % NC
    for d in range(NY):
        for o in range(NC):
            s = (y + NY - d) % NY * NC + (c + o) % NC
            turned[:, :, pl.ds(s, 1)] = parts[d][o].swapaxes(0, 1)[:, :, None]
    shards, bands, shares, part, count = turned.shape
    rows = bands * shares * part
    for j in range(shards):
        out_ref[:, j * rows : (j + 1) * rows] = turned[j].reshape(rows, count).T


def place_back(place, parts):
    cores, depth, count = parts[0].shape
    part = depth // (NX * NZ)
    step = NZ // 2
    columns = step * NX * GROUP * part
    return pl.pallas_call(
        place_kernel,
        grid=(NZ // step,),
        in_specs=[pl.BlockSpec(memory_space=pltpu.SMEM)]
        + [pl.BlockSpec((cores, NX, step, part, count), lambda j: (0, 0, j, 0, 0))] * NY,
        out_specs=pl.BlockSpec((count, columns), lambda j: (0, j)),
        out_shape=jax.ShapeDtypeStruct((count, NZ // step * columns), BF16),
        scratch_shapes=[pltpu.VMEM((step, NX, GROUP, part, count), BF16)],
        compiler_params=params(60),
        cost_estimate=pl.CostEstimate(
            flops=0, bytes_accessed=4 * NY * cores * depth * count, transcendentals=0
        ),
        name="place_back",
    )(place, *[p.reshape(cores, NX, NZ, part, count) for p in parts])


def sum_kernel(parts_ref, out_ref):
    out_ref[...] = jnp.sum(parts_ref[...].astype(F32), axis=0).astype(BF16)


def turn_kernel(parts_ref, out_ref):
    near, far = out_ref.shape[:2]
    for jl in range(near):
        for jh in range(far):
            out_ref[jl, jh] = jnp.sum(parts_ref[:, jh * near + jl].astype(F32), axis=0).astype(BF16)


def sum_parts(parts, kernel, shape, name):
    return pl.pallas_call(
        kernel,
        out_shape=jax.ShapeDtypeStruct(shape, BF16),
        compiler_params=params(40),
        name=name,
    )(parts)


def copy_kernel(parts_ref, out_ref):
    total = jnp.sum(parts_ref[...].astype(F32), axis=0).astype(BF16)
    out_ref[...] = jnp.broadcast_to(total[None], out_ref.shape)


def exchange(parts, axes):
    return lax.all_to_all(parts, axes, split_axis=0, concat_axis=0, tiled=True)


def body(tokens, weight, target, bounds, kept):
    count, model = tokens.shape
    shard_rows, width = weight.shape
    tiles = shard_rows // TILE_ROWS
    scale = 1.0 / math.sqrt(count * NZ * OWNERS)
    part = shard_rows // OWNERS
    group = ("y", "c")
    place = lax.axis_index(group).reshape(1)
    core = lax.axis_index("c").reshape(1)
    y = lax.axis_index("y").reshape(1)
    swap = [(0, 1), (1, 0)]

    cut, packed = cut_tokens(place, tokens, weight, kept.reshape(-1))
    features = exchange(cut, group).reshape(NY, NC, model // GROUP, count)
    packed = lax.all_gather(packed, ("zh", "zl"), axis=0, tiled=False)

    other = forward_parts(1 - core, features, packed, BF16, NZ, "forward_other")
    got = lax.ppermute(other, "c", swap)
    own = forward_parts(core, features, packed, F32, 0, "forward_own")
    outputs = exchange(join_parts(core, own, got, packed), "y")
    own = exchange(sum_errors(outputs, target), "y").reshape(-1, width)
    masked = mask_features(place, features, outputs)
    own, masked = lax.optimization_barrier((own, masked))
    other = lax.ppermute(own, "c", swap)

    parts = grad_parts(masked, own, other, scale)
    parts, own, other, packed = lax.optimization_barrier((parts, own, other, packed))
    parts = exchange(parts.reshape(NX, NZ, part, width), "x")

    got = lax.ppermute(back_parts(y, other, packed), "c", swap)
    back = back_parts(y, own, packed, got)
    parts = exchange(sum_parts(parts, turn_kernel, (NL, NH, part, width), "sum_x"), "zl")
    parts, back = lax.optimization_barrier((parts, back))
    back = [
        back[d] if d == 0 else lax.ppermute(back[d], "y", [(k, (k + d) % NY) for k in range(NY)])
        for d in range(NY)
    ]
    inputs_grad = place_back(place, back)

    parts = exchange(sum_parts(parts, sum_kernel, (NH, part, width), "sum_near"), "zh")
    parts = sum_parts(parts, copy_kernel, (OWNERS, part, width), "sum_far")
    selected = exchange(parts, ("x", *group)).reshape(shard_rows, width)

    first, last = bounds[0, 0, 0], bounds[0, 0, 1]
    slots = []
    for s in range(3 * tiles // (2 * OWNERS)):
        at = jnp.minimum(first + s, tiles - 1) * TILE_ROWS
        tile = lax.dynamic_slice_in_dim(selected, at, TILE_ROWS, 0).astype(F32)
        slots.append(jnp.where(s < last - first, tile, 0.0).reshape(-1))
    return inputs_grad, selected, jnp.stack(slots)[None, None]


def solution(mesh):
    fine = Mesh(mesh.devices.reshape(NX, NY, NC, NH, NL), ("x", "y", "c", "zh", "zl"))
    dp, fsdp = ("x", "y", "c"), ("zh", "zl")
    return jax.shard_map(
        body,
        mesh=fine,
        in_specs=(
            P((*dp, *fsdp), None),
            P(fsdp, None),
            P((*dp, *fsdp), None),
            P(fsdp, dp, None),
            P(dp, fsdp, None),
        ),
        out_specs=(P((*dp, *fsdp), None), P(fsdp, None), P(fsdp, dp, None, None)),
        check_vma=False,
    )
```

```python
import functools
import math

import jax
import jax.numpy as jnp
from jax import lax
from jax.experimental import pallas as pl
from jax.experimental.pallas import tpu as pltpu
from jax.sharding import Mesh, PartitionSpec as P

TILE_ROWS = 8
NX, NY, NC, NZ = 4, 4, 2, 16
GROUP = NY * NC
OWNERS = NX * GROUP
F32, BF16 = jnp.float32, jnp.bfloat16
VMEM_MB = 1024 * 1024
LANES = 128


def params(megabytes):
    return pltpu.CompilerParams(vmem_limit_bytes=megabytes * VMEM_MB)


def cut_kernel(place_ref, tok_ref, weight_ref, kept_ref, out_ref, packed_ref):
    shares, bands, shards, part, count = out_ref.shape
    rows = bands * shares * part
    for j in range(shards):
        turned = tok_ref[:, j * rows : (j + 1) * rows].T
        out_ref[:, :, j] = turned.reshape(bands, shares, part, count).swapaxes(0, 1)

    @pl.when(pl.program_id(0) == 0)
    def _():
        rows = bands * part
        blocks = weight_ref.shape[3] // LANES
        for b in range(blocks):
            block = weight_ref[:, 0, :, b * LANES : (b + 1) * LANES]
            packed_ref[b * rows : (b + 1) * rows] = block.reshape(rows, LANES)
        lane = lax.broadcasted_iota(jnp.int32, (part, LANES), 1)
        hits = jnp.zeros((part, LANES), F32)
        for k in range(kept_ref.shape[0]):
            hits = jnp.where(lane == kept_ref[k], 1.0, hits)
        first = lax.broadcasted_iota(jnp.int32, (part, LANES), 0) == 0
        packed_ref[blocks * rows :] = jnp.where(first, hits, 0.0).astype(BF16)


def cut_tokens(place, tokens, weight, kept):
    count, model = tokens.shape
    rows = model // NZ
    part = rows // OWNERS
    width = weight.shape[1]
    packed = (NX * width // LANES + 1) * part
    step = NZ // 2
    return pl.pallas_call(
        cut_kernel,
        grid_spec=pltpu.PrefetchScalarGridSpec(
            num_scalar_prefetch=1,
            grid=(NZ // step,),
            in_specs=[
                pl.BlockSpec((count, rows * step), lambda j, at: (0, j)),
                pl.BlockSpec((NX, 1, part, width), lambda j, at: (0, at[0], 0, 0)),
                pl.BlockSpec(memory_space=pltpu.SMEM),
            ],
            out_specs=[
                pl.BlockSpec((GROUP, NX, step, part, count), lambda j, at: (0, 0, j, 0, 0)),
                pl.BlockSpec((packed, LANES), lambda j, at: (0, 0)),
            ],
        ),
        out_shape=[
            jax.ShapeDtypeStruct((GROUP, NX, NZ, part, count), BF16),
            jax.ShapeDtypeStruct((packed, LANES), BF16),
        ],
        compiler_params=params(60),
        cost_estimate=pl.CostEstimate(flops=0, bytes_accessed=4 * count * model, transcendentals=0),
        name="cut_tokens",
    )(place, tokens, weight.reshape(NX, GROUP, part, width), kept)


def unpack_rows(packed_ref, rows):
    bands, _, part, width = rows.shape
    for b in range(width // LANES):
        for x in range(bands):
            at = (b * bands + x) * part
            rows[x, :, :, b * LANES : (b + 1) * LANES] = packed_ref[:, at : at + part, :]


def forward_kernel(core_ref, feat_ref, packed_ref, out_ref, rows):
    width = rows.shape[3]
    count = feat_ref.shape[3]

    @pl.when(pl.program_id(0) == 0)
    def _():
        unpack_rows(packed_ref, rows)

    out_ref[0, :count] = lax.dot_general(
        feat_ref[0, 0],
        rows[...].reshape(-1, width),
        (((0,), (0,)), ((), ())),
        preferred_element_type=F32,
    ).astype(out_ref.dtype)
    if out_ref.shape[1] > count:
        out_ref[0, count:] = jnp.zeros((out_ref.shape[1] - count, width), BF16)
        out_ref[0, count:, :LANES] = read_hits(packed_ref[:, NX * rows.shape[2] * width // LANES :, :])


def read_hits(block):
    return jnp.sum(block.astype(F32), axis=1).astype(BF16)


def forward_parts(core, features, packed, kind, extra, name):
    members, _, depth, count = features.shape
    shards, block, _ = packed.shape
    part = depth // (NX * shards)
    width = (block // part - 1) // NX * LANES
    return pl.pallas_call(
        forward_kernel,
        grid_spec=pltpu.PrefetchScalarGridSpec(
            num_scalar_prefetch=1,
            grid=(members,),
            in_specs=[
                pl.BlockSpec((1, 1, depth, count), lambda i, at: (i, at[0], 0, 0)),
                pl.BlockSpec((shards, block, LANES), lambda i, at: (0, 0, 0)),
            ],
            out_specs=pl.BlockSpec((1, count + extra, width), lambda i, at: (i, 0, 0)),
            scratch_shapes=[pltpu.VMEM((NX, shards, part, width), BF16)],
        ),
        out_shape=jax.ShapeDtypeStruct((members, count + extra, width), kind),
        compiler_params=params(40),
        cost_estimate=pl.CostEstimate(
            flops=2 * members * depth * count * width,
            bytes_accessed=2 * (members * count * (depth + width) + depth * width),
            transcendentals=0,
        ),
        name=name,
    )(core, features, packed)


def join_kernel(core_ref, own_ref, got_ref, packed_ref, out_ref):
    count = own_ref.shape[1]
    shards = packed_ref.shape[0]
    out_ref[:, :count] = (own_ref[...] + got_ref[:, :count, :].astype(F32)).astype(BF16)
    mine = read_hits(packed_ref[...]).astype(F32)
    other = got_ref[0, count:, :LANES].astype(F32)
    members, _, width = got_ref.shape
    for c in range(NC):
        at = slice(count + c * shards, count + (c + 1) * shards)
        hits = jnp.where(core_ref[0] == c, mine, other).astype(BF16)
        out_ref[:, at] = jnp.zeros((members, shards, width), BF16)
        out_ref[:, at, :LANES] = jnp.broadcast_to(hits[None], (members, shards, LANES))


def join_parts(core, own, got, packed):
    members, count, width = own.shape
    shards, block, _ = packed.shape
    part = got.shape[1] - count
    return pl.pallas_call(
        join_kernel,
        grid=(1,),
        in_specs=[
            pl.BlockSpec(memory_space=pltpu.SMEM),
            pl.BlockSpec(own.shape, lambda i: (0, 0, 0)),
            pl.BlockSpec(got.shape, lambda i: (0, 0, 0)),
            pl.BlockSpec((shards, part, LANES), lambda i: (0, block // part - 1, 0)),
        ],
        out_specs=pl.BlockSpec((members, count + NC * shards, width), lambda i: (0, 0, 0)),
        out_shape=jax.ShapeDtypeStruct((members, count + NC * shards, width), BF16),
        compiler_params=params(40),
        name="join_parts",
    )(core, own, got, packed)


def error_kernel(parts_ref, target_ref, copies_ref):
    count = target_ref.shape[0]
    outputs = jnp.sum(parts_ref[:, :count, :].astype(F32), axis=0)
    errors = (outputs - target_ref[...].astype(F32)).astype(BF16)
    copies_ref[...] = jnp.broadcast_to(errors[None], copies_ref.shape)


def sum_errors(parts, target):
    return pl.pallas_call(
        error_kernel,
        out_shape=jax.ShapeDtypeStruct((parts.shape[0], *target.shape), BF16),
        compiler_params=params(40),
        name="sum_errors",
    )(parts, target)


def mask_kernel(place_ref, feat_ref, hits_ref, out_ref):
    members, _, depth, count = feat_ref.shape
    shards, lanes = hits_ref.shape[1:]
    part = depth // (NX * shards)
    each = part // TILE_ROWS
    row = lax.broadcasted_iota(jnp.int32, (depth, shards), 0)
    at = lax.broadcasted_iota(jnp.int32, (depth, shards), 1)
    shard = ((row // part) % shards == at).astype(BF16)
    row = lax.broadcasted_iota(jnp.int32, (depth, lanes), 0)
    at = lax.broadcasted_iota(jnp.int32, (depth, lanes), 1)
    tile = (row // (part * shards) * GROUP + place_ref[0]) * each + row // TILE_ROWS % each
    ones = jnp.ones((lanes, count), BF16)
    for y in range(members):
        hits = jnp.dot(shard, hits_ref[y], preferred_element_type=F32)
        hits = jnp.where(tile == at, hits, 0.0).astype(BF16)
        keep = jnp.dot(hits, ones, preferred_element_type=F32)
        out_ref[0, y] = feat_ref[y, 0] * keep.astype(BF16)


def mask_features(place, features, parts):
    members, cores, depth, count = features.shape
    return pl.pallas_call(
        mask_kernel,
        grid_spec=pltpu.PrefetchScalarGridSpec(
            num_scalar_prefetch=1,
            grid=(cores,),
            in_specs=[
                pl.BlockSpec((members, 1, depth, count), lambda o, at: (0, (o + at[0]) % NC, 0, 0)),
                pl.BlockSpec((members, NZ, LANES), lambda o, at: (0, count // NZ + (o + at[0]) % NC, 0)),
            ],
            out_specs=pl.BlockSpec((1, members, depth, count), lambda o, at: (o, 0, 0, 0)),
        ),
        out_shape=jax.ShapeDtypeStruct((cores, members, depth, count), BF16),
        compiler_params=params(60),
        cost_estimate=pl.CostEstimate(
            flops=2 * cores * members * depth * LANES * (NZ + count),
            bytes_accessed=4 * cores * members * depth * count,
            transcendentals=0,
        ),
        name="mask_features",
    )(place, features, parts)


def grad_kernel(scale, feat_ref, own_ref, other_ref, out_ref):
    total = 0.0
    for o, errors in enumerate((own_ref, other_ref)):
        features = jnp.concatenate([feat_ref[o, y] for y in range(feat_ref.shape[1])], axis=1)
        total += jnp.dot(features, errors[...], preferred_element_type=F32)
    out_ref[...] = (total * scale).astype(BF16)


def grad_parts(features, own, other, scale):
    cores, members, depth, count = features.shape
    both, width = own.shape
    step = depth // 2
    return pl.pallas_call(
        functools.partial(grad_kernel, scale),
        grid=(depth // step,),
        in_specs=[
            pl.BlockSpec((cores, members, step, count), lambda i: (0, 0, i, 0)),
            pl.BlockSpec((both, width), lambda i: (0, 0)),
            pl.BlockSpec((both, width), lambda i: (0, 0)),
        ],
        out_specs=pl.BlockSpec((step, width), lambda i: (i, 0)),
        out_shape=jax.ShapeDtypeStruct((depth, width), BF16),
        compiler_params=params(60),
        cost_estimate=pl.CostEstimate(
            flops=2 * depth * cores * both * width,
            bytes_accessed=2 * (cores * both * (depth + width) + depth * width),
            transcendentals=0,
        ),
        name="grad_parts",
    )(features, own, other)


def back_kernel(y_ref, err_ref, own_ref, other_ref, *outs_and_rows):
    outs, rows = outs_and_rows[:-1], outs_and_rows[-1]
    count = err_ref.shape[0] // NY
    for o, packed in enumerate((own_ref, other_ref)):
        unpack_rows(packed, rows.at[o])
    for d in range(NY):
        at = pl.multiple_of((y_ref[0] + d) % NY * count, count)
        for o in range(NC):
            outs[d][o] = lax.dot_general(
                rows[o].reshape(-1, rows.shape[4]),
                err_ref[pl.ds(at, count), :],
                (((1,), (1,)), ((), ())),
                preferred_element_type=F32,
            ).astype(BF16)


def back_parts(y, errors, own, other):
    shards, block, _ = own.shape
    both, width = errors.shape
    part = block // (NX * width // LANES + 1)
    depth, count = NX * shards * part, both // NY
    return pl.pallas_call(
        back_kernel,
        in_specs=[pl.BlockSpec(memory_space=pltpu.SMEM)] + [pl.BlockSpec(memory_space=pltpu.VMEM)] * 3,
        out_shape=[jax.ShapeDtypeStruct((NC, depth, count), BF16)] * NY,
        scratch_shapes=[pltpu.VMEM((NC, NX, shards, part, width), BF16)],
        compiler_params=params(40),
        cost_estimate=pl.CostEstimate(
            flops=2 * NC * depth * both * width,
            bytes_accessed=2 * NC * depth * (both + width),
            transcendentals=0,
        ),
        name="back_parts",
    )(y, errors, own, other)


def place_kernel(place_ref, *refs):
    parts, out_ref, turned = refs[:NY], refs[NY], refs[NY + 1]
    y, c = place_ref[0] // NC, place_ref[0] % NC
    for d in range(NY):
        for o in range(NC):
            s = (y + NY - d) % NY * NC + (c + o) % NC
            turned[:, :, pl.ds(s, 1)] = parts[d][o].swapaxes(0, 1)[:, :, None]
    shards, bands, shares, part, count = turned.shape
    rows = bands * shares * part
    for j in range(shards):
        out_ref[:, j * rows : (j + 1) * rows] = turned[j].reshape(rows, count).T


def place_back(place, parts):
    cores, depth, count = parts[0].shape
    part = depth // (NX * NZ)
    step = NZ // 2
    columns = step * NX * GROUP * part
    return pl.pallas_call(
        place_kernel,
        grid=(NZ // step,),
        in_specs=[pl.BlockSpec(memory_space=pltpu.SMEM)]
        + [pl.BlockSpec((cores, NX, step, part, count), lambda j: (0, 0, j, 0, 0))] * NY,
        out_specs=pl.BlockSpec((count, columns), lambda j: (0, j)),
        out_shape=jax.ShapeDtypeStruct((count, NZ // step * columns), BF16),
        scratch_shapes=[pltpu.VMEM((step, NX, GROUP, part, count), BF16)],
        compiler_params=params(40),
        cost_estimate=pl.CostEstimate(
            flops=0, bytes_accessed=4 * NY * cores * depth * count, transcendentals=0
        ),
        name="place_back",
    )(place, *[p.reshape(cores, NX, NZ, part, count) for p in parts])


def sum_kernel(parts_ref, out_ref):
    out_ref[...] = jnp.sum(parts_ref[...].astype(F32), axis=0).astype(BF16)


def sum_parts(parts, kernel, shape, name):
    return pl.pallas_call(
        kernel,
        out_shape=jax.ShapeDtypeStruct(shape, BF16),
        compiler_params=params(40),
        name=name,
    )(parts)


def copy_kernel(parts_ref, out_ref):
    total = jnp.sum(parts_ref[...].astype(F32), axis=0).astype(BF16)
    out_ref[...] = jnp.broadcast_to(total[None], out_ref.shape)


def exchange(parts, axes):
    return lax.all_to_all(parts, axes, split_axis=0, concat_axis=0, tiled=True)


def body(tokens, weight, target, bounds, kept):
    count, model = tokens.shape
    shard_rows, width = weight.shape
    tiles = shard_rows // TILE_ROWS
    scale = 1.0 / math.sqrt(count * NZ * OWNERS)
    part = shard_rows // OWNERS
    group = ("y", "c")
    place = lax.axis_index(group).reshape(1)
    core = lax.axis_index("c").reshape(1)
    y = lax.axis_index("y").reshape(1)
    swap = [(0, 1), (1, 0)]

    cut, packed = cut_tokens(place, tokens, weight, kept.reshape(-1))
    features = exchange(cut, group).reshape(NY, NC, model // GROUP, count)
    packed = lax.all_gather(packed, "z", axis=0, tiled=False)

    other = forward_parts(1 - core, features, packed, BF16, NZ, "forward_other")
    got = lax.ppermute(other, "c", swap)
    own = forward_parts(core, features, packed, F32, 0, "forward_own")
    outputs = exchange(join_parts(core, own, got, packed), "y")
    own = exchange(sum_errors(outputs, target), "y").reshape(-1, width)
    masked = mask_features(place, features, outputs)
    masked, packed = lax.optimization_barrier((masked, packed))
    turned = lax.ppermute(packed, "c", swap)
    own, masked = lax.optimization_barrier((own, masked))
    other = lax.ppermute(own, "c", swap)

    parts = grad_parts(masked, own, other, scale)
    parts, own = lax.optimization_barrier((parts, own))
    parts = exchange(parts.reshape(NX, NZ, part, width), "x")

    back = back_parts(y, own, packed, turned)
    parts, back = lax.optimization_barrier((parts, back))
    back = [
        back[d] if d == 0 else lax.ppermute(back[d], "y", [(k, (k + d) % NY) for k in range(NY)])
        for d in range(NY)
    ]
    inputs_grad = place_back(place, back)

    parts = exchange(sum_parts(parts, sum_kernel, (NZ, part, width), "sum_x"), "z")
    parts = sum_parts(parts, copy_kernel, (OWNERS, part, width), "sum_z")
    selected = exchange(parts, ("x", *group)).reshape(shard_rows, width)

    first, last = bounds[0, 0, 0], bounds[0, 0, 1]
    slots = []
    for s in range(3 * tiles // (2 * OWNERS)):
        at = jnp.minimum(first + s, tiles - 1) * TILE_ROWS
        tile = lax.dynamic_slice_in_dim(selected, at, TILE_ROWS, 0).astype(F32)
        slots.append(jnp.where(s < last - first, tile, 0.0).reshape(-1))
    return inputs_grad, selected, jnp.stack(slots)[None, None]


def solution(mesh):
    fine = Mesh(mesh.devices.reshape(NX, NY, NC, NZ), ("x", "y", "c", "z"))
    dp = ("x", "y", "c")
    return jax.shard_map(
        body,
        mesh=fine,
        in_specs=(
            P((*dp, "z"), None),
            P("z", None),
            P((*dp, "z"), None),
            P("z", dp, None),
            P(dp, "z", None),
        ),
        out_specs=(P((*dp, "z"), None), P("z", None), P("z", dp, None, None)),
        check_vma=False,
    )
```

```python
import functools
import math

import jax
import jax.numpy as jnp
from jax import lax
from jax.experimental import pallas as pl
from jax.experimental.pallas import tpu as pltpu
from jax.sharding import Mesh, PartitionSpec as P

TILE_ROWS = 8
NX, NY, NC, NZ = 4, 4, 2, 16
GROUP = NY * NC
OWNERS = NX * GROUP
F32, BF16 = jnp.float32, jnp.bfloat16
VMEM_MB = 1024 * 1024
LANES = 128


def params(megabytes):
    return pltpu.CompilerParams(vmem_limit_bytes=megabytes * VMEM_MB)


def cut_kernel(place_ref, tok_ref, weight_ref, kept_ref, out_ref, packed_ref):
    shares, bands, shards, part, count = out_ref.shape
    rows = bands * shares * part
    for j in range(shards):
        turned = tok_ref[:, j * rows : (j + 1) * rows].T
        out_ref[:, :, j] = turned.reshape(bands, shares, part, count).swapaxes(0, 1)

    @pl.when(pl.program_id(0) == 0)
    def _():
        rows = bands * part
        blocks = weight_ref.shape[3] // LANES
        for b in range(blocks):
            block = weight_ref[:, 0, :, b * LANES : (b + 1) * LANES]
            packed_ref[b * rows : (b + 1) * rows] = block.reshape(rows, LANES)
        lane = lax.broadcasted_iota(jnp.int32, (part, LANES), 1)
        hits = jnp.zeros((part, LANES), F32)
        for k in range(kept_ref.shape[0]):
            hits = jnp.where(lane == kept_ref[k], 1.0, hits)
        first = lax.broadcasted_iota(jnp.int32, (part, LANES), 0) == 0
        packed_ref[blocks * rows :] = jnp.where(first, hits, 0.0).astype(BF16)


def cut_tokens(place, tokens, weight, kept):
    count, model = tokens.shape
    rows = model // NZ
    part = rows // OWNERS
    width = weight.shape[1]
    packed = (NX * width // LANES + 1) * part
    step = NZ // 2
    return pl.pallas_call(
        cut_kernel,
        grid_spec=pltpu.PrefetchScalarGridSpec(
            num_scalar_prefetch=1,
            grid=(NZ // step,),
            in_specs=[
                pl.BlockSpec((count, rows * step), lambda j, at: (0, j)),
                pl.BlockSpec((NX, 1, part, width), lambda j, at: (0, at[0], 0, 0)),
                pl.BlockSpec(memory_space=pltpu.SMEM),
            ],
            out_specs=[
                pl.BlockSpec((GROUP, NX, step, part, count), lambda j, at: (0, 0, j, 0, 0)),
                pl.BlockSpec((packed, LANES), lambda j, at: (0, 0)),
            ],
        ),
        out_shape=[
            jax.ShapeDtypeStruct((GROUP, NX, NZ, part, count), BF16),
            jax.ShapeDtypeStruct((packed, LANES), BF16),
        ],
        compiler_params=params(60),
        cost_estimate=pl.CostEstimate(flops=0, bytes_accessed=4 * count * model, transcendentals=0),
        name="cut_tokens",
    )(place, tokens, weight.reshape(NX, GROUP, part, width), kept)


def unpack_rows(packed_ref, rows):
    bands, _, part, width = rows.shape
    for b in range(width // LANES):
        for x in range(bands):
            at = (b * bands + x) * part
            rows[x, :, :, b * LANES : (b + 1) * LANES] = packed_ref[:, at : at + part, :]


def forward_kernel(core_ref, feat_ref, packed_ref, out_ref, rows):
    width = rows.shape[3]
    count = feat_ref.shape[3]

    @pl.when(pl.program_id(0) == 0)
    def _():
        unpack_rows(packed_ref, rows)

    out_ref[0, :count] = lax.dot_general(
        feat_ref[0, 0],
        rows[...].reshape(-1, width),
        (((0,), (0,)), ((), ())),
        preferred_element_type=F32,
    ).astype(out_ref.dtype)
    if out_ref.shape[1] > count:
        out_ref[0, count:] = jnp.zeros((out_ref.shape[1] - count, width), BF16)
        out_ref[0, count:, :LANES] = read_hits(packed_ref[:, NX * rows.shape[2] * width // LANES :, :])


def read_hits(block):
    return jnp.sum(block.astype(F32), axis=1).astype(BF16)


def forward_parts(core, features, packed, kind, extra, name):
    members, _, depth, count = features.shape
    shards, block, _ = packed.shape
    part = depth // (NX * shards)
    width = (block // part - 1) // NX * LANES
    return pl.pallas_call(
        forward_kernel,
        grid_spec=pltpu.PrefetchScalarGridSpec(
            num_scalar_prefetch=1,
            grid=(members,),
            in_specs=[
                pl.BlockSpec((1, 1, depth, count), lambda i, at: (i, at[0], 0, 0)),
                pl.BlockSpec((shards, block, LANES), lambda i, at: (0, 0, 0)),
            ],
            out_specs=pl.BlockSpec((1, count + extra, width), lambda i, at: (i, 0, 0)),
            scratch_shapes=[pltpu.VMEM((NX, shards, part, width), BF16)],
        ),
        out_shape=jax.ShapeDtypeStruct((members, count + extra, width), kind),
        compiler_params=params(40),
        cost_estimate=pl.CostEstimate(
            flops=2 * members * depth * count * width,
            bytes_accessed=2 * (members * count * (depth + width) + depth * width),
            transcendentals=0,
        ),
        name=name,
    )(core, features, packed)


def join_kernel(core_ref, own_ref, got_ref, packed_ref, out_ref):
    count = own_ref.shape[1]
    shards = packed_ref.shape[0]
    out_ref[:, :count] = (own_ref[...] + got_ref[:, :count, :].astype(F32)).astype(BF16)
    mine = read_hits(packed_ref[...]).astype(F32)
    other = got_ref[0, count:, :LANES].astype(F32)
    members, _, width = got_ref.shape
    out_ref[:, count:] = jnp.zeros((members, shards, width), BF16)
    for c in range(NC):
        hits = jnp.where(core_ref[0] == c, mine, other).astype(BF16)
        out_ref[:, count:, c * LANES : (c + 1) * LANES] = jnp.broadcast_to(hits[None], (members, shards, LANES))


def join_parts(core, own, got, packed):
    members, count, width = own.shape
    shards, block, _ = packed.shape
    part = got.shape[1] - count
    return pl.pallas_call(
        join_kernel,
        grid=(1,),
        in_specs=[
            pl.BlockSpec(memory_space=pltpu.SMEM),
            pl.BlockSpec(own.shape, lambda i: (0, 0, 0)),
            pl.BlockSpec(got.shape, lambda i: (0, 0, 0)),
            pl.BlockSpec((shards, part, LANES), lambda i: (0, block // part - 1, 0)),
        ],
        out_specs=pl.BlockSpec((members, count + shards, width), lambda i: (0, 0, 0)),
        out_shape=jax.ShapeDtypeStruct((members, count + shards, width), BF16),
        compiler_params=params(40),
        name="join_parts",
    )(core, own, got, packed)


def error_kernel(parts_ref, target_ref, copies_ref):
    count = target_ref.shape[0]
    outputs = jnp.sum(parts_ref[:, :count, :].astype(F32), axis=0)
    errors = (outputs - target_ref[...].astype(F32)).astype(BF16)
    copies_ref[...] = jnp.broadcast_to(errors[None], copies_ref.shape)


def sum_errors(parts, target):
    return pl.pallas_call(
        error_kernel,
        out_shape=jax.ShapeDtypeStruct((parts.shape[0], *target.shape), BF16),
        compiler_params=params(40),
        name="sum_errors",
    )(parts, target)


def mask_kernel(place_ref, feat_ref, hits_ref, out_ref):
    members, _, depth, count = feat_ref.shape
    shards, lanes = hits_ref.shape[1:]
    part = depth // (NX * shards)
    each = part // TILE_ROWS
    row = lax.broadcasted_iota(jnp.int32, (depth, shards), 0)
    at = lax.broadcasted_iota(jnp.int32, (depth, shards), 1)
    shard = ((row // part) % shards == at).astype(BF16)
    row = lax.broadcasted_iota(jnp.int32, (depth, lanes), 0)
    at = lax.broadcasted_iota(jnp.int32, (depth, lanes), 1)
    tile = (row // (part * shards) * GROUP + place_ref[0]) * each + row // TILE_ROWS % each
    ones = jnp.ones((lanes, count), BF16)
    for y in range(members):
        hits = jnp.dot(shard, hits_ref[y], preferred_element_type=F32)
        hits = jnp.where(tile == at, hits, 0.0).astype(BF16)
        keep = jnp.dot(hits, ones, preferred_element_type=F32)
        out_ref[0, y] = feat_ref[y, 0] * keep.astype(BF16)


def mask_features(place, features, parts):
    members, cores, depth, count = features.shape
    return pl.pallas_call(
        mask_kernel,
        grid_spec=pltpu.PrefetchScalarGridSpec(
            num_scalar_prefetch=1,
            grid=(cores,),
            in_specs=[
                pl.BlockSpec((members, 1, depth, count), lambda o, at: (0, (o + at[0]) % NC, 0, 0)),
                pl.BlockSpec((members, NZ, LANES), lambda o, at: (0, count // NZ, (o + at[0]) % NC)),
            ],
            out_specs=pl.BlockSpec((1, members, depth, count), lambda o, at: (o, 0, 0, 0)),
        ),
        out_shape=jax.ShapeDtypeStruct((cores, members, depth, count), BF16),
        compiler_params=params(60),
        cost_estimate=pl.CostEstimate(
            flops=2 * cores * members * depth * LANES * (NZ + count),
            bytes_accessed=4 * cores * members * depth * count,
            transcendentals=0,
        ),
        name="mask_features",
    )(place, features, parts)


def grad_kernel(scale, feat_ref, own_ref, other_ref, out_ref):
    total = 0.0
    for o, errors in enumerate((own_ref, other_ref)):
        features = jnp.concatenate([feat_ref[o, y] for y in range(feat_ref.shape[1])], axis=1)
        total += jnp.dot(features, errors[...], preferred_element_type=F32)
    out_ref[...] = (total * scale).astype(BF16)


def grad_parts(features, own, other, scale):
    cores, members, depth, count = features.shape
    both, width = own.shape
    step = depth // 2
    return pl.pallas_call(
        functools.partial(grad_kernel, scale),
        grid=(depth // step,),
        in_specs=[
            pl.BlockSpec((cores, members, step, count), lambda i: (0, 0, i, 0)),
            pl.BlockSpec((both, width), lambda i: (0, 0)),
            pl.BlockSpec((both, width), lambda i: (0, 0)),
        ],
        out_specs=pl.BlockSpec((step, width), lambda i: (i, 0)),
        out_shape=jax.ShapeDtypeStruct((depth, width), BF16),
        compiler_params=params(60),
        cost_estimate=pl.CostEstimate(
            flops=2 * depth * cores * both * width,
            bytes_accessed=2 * (cores * both * (depth + width) + depth * width),
            transcendentals=0,
        ),
        name="grad_parts",
    )(features, own, other)


def back_kernel(y_ref, err_ref, own_ref, other_ref, *outs_and_rows):
    outs, rows = outs_and_rows[:-1], outs_and_rows[-1]
    count = err_ref.shape[0] // NY
    for o, packed in enumerate((own_ref, other_ref)):
        unpack_rows(packed, rows.at[o])
    places = {(0, 0): (0, 0), (0, 1): (0, 1), (1, 0): (1, 0), (1, 1): (1, 1)}
    places |= {(2, 0): (1, 2), (2, 1): (2, 2), (3, 0): (2, 0), (3, 1): (2, 1)}
    for d in range(NY):
        at = pl.multiple_of((y_ref[0] + d) % NY * count, count)
        for o in range(NC):
            out, k = places[d, o]
            outs[out][k] = lax.dot_general(
                rows[o].reshape(-1, rows.shape[4]),
                err_ref[pl.ds(at, count), :],
                (((1,), (1,)), ((), ())),
                preferred_element_type=F32,
            ).astype(BF16)


def back_parts(y, errors, own, other):
    shards, block, _ = own.shape
    both, width = errors.shape
    part = block // (NX * width // LANES + 1)
    depth, count = NX * shards * part, both // NY
    return pl.pallas_call(
        back_kernel,
        in_specs=[pl.BlockSpec(memory_space=pltpu.SMEM)] + [pl.BlockSpec(memory_space=pltpu.VMEM)] * 3,
        out_shape=[jax.ShapeDtypeStruct((k, depth, count), BF16) for k in (NC, NC + 1, NC + 1)],
        scratch_shapes=[pltpu.VMEM((NC, NX, shards, part, width), BF16)],
        compiler_params=params(40),
        cost_estimate=pl.CostEstimate(
            flops=2 * NC * depth * both * width,
            bytes_accessed=2 * NC * depth * (both + width),
            transcendentals=0,
        ),
        name="back_parts",
    )(y, errors, own, other)


def place_kernel(place_ref, stay_ref, up_ref, down_ref, far_up_ref, far_down_ref, out_ref, turned):
    y, c = place_ref[0] // NC, place_ref[0] % NC
    parts = {(0, 0): (stay_ref, 0), (0, 1): (stay_ref, 1), (1, 0): (up_ref, 0), (1, 1): (up_ref, 1)}
    parts |= {(2, 0): (far_up_ref, 0), (2, 1): (far_down_ref, 0), (3, 0): (down_ref, 0), (3, 1): (down_ref, 1)}
    for (d, o), (ref, k) in parts.items():
        s = (y + NY - d) % NY * NC + (c + o) % NC
        turned[:, :, pl.ds(s, 1)] = ref[k].swapaxes(0, 1)[:, :, None]
    shards, bands, shares, part, count = turned.shape
    rows = bands * shares * part
    for j in range(shards):
        out_ref[:, j * rows : (j + 1) * rows] = turned[j].reshape(rows, count).T


def place_back(place, parts):
    _, depth, count = parts[0].shape
    part = depth // (NX * NZ)
    step = NZ // 2
    columns = step * NX * GROUP * part
    return pl.pallas_call(
        place_kernel,
        grid=(NZ // step,),
        in_specs=[pl.BlockSpec(memory_space=pltpu.SMEM)]
        + [pl.BlockSpec((p.shape[0], NX, step, part, count), lambda j: (0, 0, j, 0, 0)) for p in parts],
        out_specs=pl.BlockSpec((count, columns), lambda j: (0, j)),
        out_shape=jax.ShapeDtypeStruct((count, NZ // step * columns), BF16),
        scratch_shapes=[pltpu.VMEM((step, NX, GROUP, part, count), BF16)],
        compiler_params=params(40),
        cost_estimate=pl.CostEstimate(
            flops=0, bytes_accessed=4 * NY * NC * depth * count, transcendentals=0
        ),
        name="place_back",
    )(place, *[p.reshape(p.shape[0], NX, NZ, part, count) for p in parts])


def sum_kernel(parts_ref, out_ref):
    out_ref[...] = jnp.sum(parts_ref[...].astype(F32), axis=0).astype(BF16)


def sum_parts(parts, kernel, shape, name):
    return pl.pallas_call(
        kernel,
        out_shape=jax.ShapeDtypeStruct(shape, BF16),
        compiler_params=params(40),
        name=name,
    )(parts)


def copy_kernel(parts_ref, out_ref):
    total = jnp.sum(parts_ref[...].astype(F32), axis=0).astype(BF16)
    out_ref[...] = jnp.broadcast_to(total[None], out_ref.shape)


def exchange(parts, axes):
    return lax.all_to_all(parts, axes, split_axis=0, concat_axis=0, tiled=True)


def body(tokens, weight, target, bounds, kept):
    count, model = tokens.shape
    shard_rows, width = weight.shape
    tiles = shard_rows // TILE_ROWS
    scale = 1.0 / math.sqrt(count * NZ * OWNERS)
    part = shard_rows // OWNERS
    group = ("y", "c")
    place = lax.axis_index(group).reshape(1)
    core = lax.axis_index("c").reshape(1)
    y = lax.axis_index("y").reshape(1)
    swap = [(0, 1), (1, 0)]

    cut, packed = cut_tokens(place, tokens, weight, kept.reshape(-1))
    features = exchange(cut, group).reshape(NY, NC, model // GROUP, count)
    packed = lax.all_gather(packed, "z", axis=0, tiled=False)

    other = forward_parts(1 - core, features, packed, BF16, NZ, "forward_other")
    got = lax.ppermute(other, "c", swap)
    own = forward_parts(core, features, packed, F32, 0, "forward_own")
    outputs = exchange(join_parts(core, own, got, packed), "y")
    own = exchange(sum_errors(outputs, target), "y").reshape(-1, width)
    masked = mask_features(place, features, outputs)
    masked, packed = lax.optimization_barrier((masked, packed))
    turned = lax.ppermute(packed, "c", swap)
    own, masked = lax.optimization_barrier((own, masked))
    other = lax.ppermute(own, "c", swap)

    parts = grad_parts(masked, own, other, scale)
    parts, own = lax.optimization_barrier((parts, own))
    parts = exchange(parts.reshape(NX, NZ, part, width), "x")

    up, down = [(k, (k + 1) % NY) for k in range(NY)], [(k, (k + NY - 1) % NY) for k in range(NY)]
    stay, to_up, to_down = back_parts(y, own, packed, turned)
    parts, _, _ = lax.optimization_barrier((parts, to_up, to_down))
    from_down = lax.ppermute(to_up, "y", up)
    from_up = lax.ppermute(to_down, "y", down)
    far_down = lax.ppermute(from_down[NC:], "y", up)
    far_up = lax.ppermute(from_up[NC:], "y", down)

    parts = exchange(sum_parts(parts, sum_kernel, (NZ, part, width), "sum_x"), "z")
    parts, *_ = lax.optimization_barrier((parts, far_down, far_up))
    inputs_grad = place_back(place, [stay, from_down, from_up, far_down, far_up])
    parts = sum_parts(parts, copy_kernel, (OWNERS, part, width), "sum_z")
    selected = exchange(parts, ("x", *group)).reshape(shard_rows, width)

    first, last = bounds[0, 0, 0], bounds[0, 0, 1]
    slots = []
    for s in range(3 * tiles // (2 * OWNERS)):
        at = jnp.minimum(first + s, tiles - 1) * TILE_ROWS
        tile = lax.dynamic_slice_in_dim(selected, at, TILE_ROWS, 0).astype(F32)
        slots.append(jnp.where(s < last - first, tile, 0.0).reshape(-1))
    return inputs_grad, selected, jnp.stack(slots)[None, None]


def solution(mesh):
    fine = Mesh(mesh.devices.reshape(NX, NY, NC, NZ), ("x", "y", "c", "z"))
    dp = ("x", "y", "c")
    return jax.shard_map(
        body,
        mesh=fine,
        in_specs=(
            P((*dp, "z"), None),
            P("z", None),
            P((*dp, "z"), None),
            P("z", dp, None),
            P(dp, "z", None),
        ),
        out_specs=(P((*dp, "z"), None), P("z", None), P("z", dp, None, None)),
        check_vma=False,
    )
```

```python
import functools
import math

import jax
import jax.numpy as jnp
from jax import lax
from jax.experimental import pallas as pl
from jax.experimental.pallas import tpu as pltpu
from jax.sharding import Mesh, PartitionSpec as P

TILE_ROWS = 8
NX, NY, NC, NZ = 4, 4, 2, 16
GROUP = NY * NC
OWNERS = NX * GROUP
F32, BF16 = jnp.float32, jnp.bfloat16
VMEM_MB = 1024 * 1024
LANES = 128


def params(megabytes):
    return pltpu.CompilerParams(vmem_limit_bytes=megabytes * VMEM_MB)


def cut_kernel(place_ref, tok_ref, weight_ref, kept_ref, out_ref, packed_ref):
    shares, bands, shards, part, count = out_ref.shape
    rows = bands * shares * part
    for j in range(shards):
        turned = tok_ref[:, j * rows : (j + 1) * rows].T
        out_ref[:, :, j] = turned.reshape(bands, shares, part, count).swapaxes(0, 1)

    @pl.when(pl.program_id(0) == 0)
    def _():
        rows = bands * part
        blocks = weight_ref.shape[3] // LANES
        for b in range(blocks):
            block = weight_ref[:, 0, :, b * LANES : (b + 1) * LANES]
            packed_ref[b * rows : (b + 1) * rows] = block.reshape(rows, LANES)
        lane = lax.broadcasted_iota(jnp.int32, (part, LANES), 1)
        hits = jnp.zeros((part, LANES), F32)
        for k in range(kept_ref.shape[0]):
            hits = jnp.where(lane == kept_ref[k], 1.0, hits)
        first = lax.broadcasted_iota(jnp.int32, (part, LANES), 0) == 0
        packed_ref[blocks * rows :] = jnp.where(first, hits, 0.0).astype(BF16)


def cut_tokens(place, tokens, weight, kept):
    count, model = tokens.shape
    rows = model // NZ
    part = rows // OWNERS
    width = weight.shape[1]
    packed = (NX * width // LANES + 1) * part
    step = NZ // 2
    return pl.pallas_call(
        cut_kernel,
        grid_spec=pltpu.PrefetchScalarGridSpec(
            num_scalar_prefetch=1,
            grid=(NZ // step,),
            in_specs=[
                pl.BlockSpec((count, rows * step), lambda j, at: (0, j)),
                pl.BlockSpec((NX, 1, part, width), lambda j, at: (0, at[0], 0, 0)),
                pl.BlockSpec(memory_space=pltpu.SMEM),
            ],
            out_specs=[
                pl.BlockSpec((GROUP, NX, step, part, count), lambda j, at: (0, 0, j, 0, 0)),
                pl.BlockSpec((packed, LANES), lambda j, at: (0, 0)),
            ],
        ),
        out_shape=[
            jax.ShapeDtypeStruct((GROUP, NX, NZ, part, count), BF16),
            jax.ShapeDtypeStruct((packed, LANES), BF16),
        ],
        compiler_params=params(60),
        cost_estimate=pl.CostEstimate(flops=0, bytes_accessed=4 * count * model, transcendentals=0),
        name="cut_tokens",
    )(place, tokens, weight.reshape(NX, GROUP, part, width), kept)


def unpack_rows(packed_ref, rows):
    bands, _, part, width = rows.shape
    for b in range(width // LANES):
        for x in range(bands):
            at = (b * bands + x) * part
            rows[x, :, :, b * LANES : (b + 1) * LANES] = packed_ref[:, at : at + part, :]


def forward_kernel(core_ref, feat_ref, packed_ref, out_ref, rows):
    width = rows.shape[3]
    count = feat_ref.shape[3]

    @pl.when(pl.program_id(0) == 0)
    def _():
        unpack_rows(packed_ref, rows)

    out_ref[0, :count] = lax.dot_general(
        feat_ref[0, 0],
        rows[...].reshape(-1, width),
        (((0,), (0,)), ((), ())),
        preferred_element_type=F32,
    ).astype(out_ref.dtype)
    if out_ref.shape[1] > count:
        out_ref[0, count:] = jnp.zeros((out_ref.shape[1] - count, width), BF16)
        out_ref[0, count:, :LANES] = read_hits(packed_ref[:, NX * rows.shape[2] * width // LANES :, :])


def read_hits(block):
    return jnp.sum(block.astype(F32), axis=1).astype(BF16)


def forward_parts(core, features, packed, kind, extra, name):
    members, _, depth, count = features.shape
    shards, block, _ = packed.shape
    part = depth // (NX * shards)
    width = (block // part - 1) // NX * LANES
    return pl.pallas_call(
        forward_kernel,
        grid_spec=pltpu.PrefetchScalarGridSpec(
            num_scalar_prefetch=1,
            grid=(members,),
            in_specs=[
                pl.BlockSpec((1, 1, depth, count), lambda i, at: (i, at[0], 0, 0)),
                pl.BlockSpec((shards, block, LANES), lambda i, at: (0, 0, 0)),
            ],
            out_specs=pl.BlockSpec((1, count + extra, width), lambda i, at: (i, 0, 0)),
            scratch_shapes=[pltpu.VMEM((NX, shards, part, width), BF16)],
        ),
        out_shape=jax.ShapeDtypeStruct((members, count + extra, width), kind),
        compiler_params=params(40),
        cost_estimate=pl.CostEstimate(
            flops=2 * members * depth * count * width,
            bytes_accessed=2 * (members * count * (depth + width) + depth * width),
            transcendentals=0,
        ),
        name=name,
    )(core, features, packed)


def join_kernel(core_ref, own_ref, got_ref, packed_ref, out_ref):
    count = own_ref.shape[1]
    shards = packed_ref.shape[0]
    out_ref[:, :count] = (own_ref[...] + got_ref[:, :count, :].astype(F32)).astype(BF16)
    mine = read_hits(packed_ref[...]).astype(F32)
    other = got_ref[0, count:, :LANES].astype(F32)
    members, _, width = got_ref.shape
    out_ref[:, count:] = jnp.zeros((members, shards, width), BF16)
    for c in range(NC):
        hits = jnp.where(core_ref[0] == c, mine, other).astype(BF16)
        out_ref[:, count:, c * LANES : (c + 1) * LANES] = jnp.broadcast_to(hits[None], (members, shards, LANES))


def join_parts(core, own, got, packed):
    members, count, width = own.shape
    shards, block, _ = packed.shape
    part = got.shape[1] - count
    return pl.pallas_call(
        join_kernel,
        grid=(1,),
        in_specs=[
            pl.BlockSpec(memory_space=pltpu.SMEM),
            pl.BlockSpec(own.shape, lambda i: (0, 0, 0)),
            pl.BlockSpec(got.shape, lambda i: (0, 0, 0)),
            pl.BlockSpec((shards, part, LANES), lambda i: (0, block // part - 1, 0)),
        ],
        out_specs=pl.BlockSpec((members, count + shards, width), lambda i: (0, 0, 0)),
        out_shape=jax.ShapeDtypeStruct((members, count + shards, width), BF16),
        compiler_params=params(40),
        name="join_parts",
    )(core, own, got, packed)


def error_kernel(parts_ref, target_ref, copies_ref):
    count = target_ref.shape[0]
    outputs = jnp.sum(parts_ref[:, :count, :].astype(F32), axis=0)
    errors = (outputs - target_ref[...].astype(F32)).astype(BF16)
    copies_ref[...] = jnp.broadcast_to(errors[None], copies_ref.shape)


def sum_errors(parts, target):
    return pl.pallas_call(
        error_kernel,
        out_shape=jax.ShapeDtypeStruct((parts.shape[0], *target.shape), BF16),
        compiler_params=params(40),
        name="sum_errors",
    )(parts, target)


def mask_kernel(place_ref, feat_ref, hits_ref, out_ref):
    members, _, depth, count = feat_ref.shape
    shards, lanes = hits_ref.shape[1:]
    part = depth // (NX * shards)
    each = part // TILE_ROWS
    row = lax.broadcasted_iota(jnp.int32, (depth, shards), 0)
    at = lax.broadcasted_iota(jnp.int32, (depth, shards), 1)
    shard = ((row // part) % shards == at).astype(BF16)
    row = lax.broadcasted_iota(jnp.int32, (depth, lanes), 0)
    at = lax.broadcasted_iota(jnp.int32, (depth, lanes), 1)
    tile = (row // (part * shards) * GROUP + place_ref[0]) * each + row // TILE_ROWS % each
    ones = jnp.ones((lanes, count), BF16)
    for y in range(members):
        hits = jnp.dot(shard, hits_ref[y], preferred_element_type=F32)
        hits = jnp.where(tile == at, hits, 0.0).astype(BF16)
        keep = jnp.dot(hits, ones, preferred_element_type=F32)
        out_ref[0, y] = feat_ref[y, 0] * keep.astype(BF16)


def mask_features(place, features, parts):
    members, cores, depth, count = features.shape
    return pl.pallas_call(
        mask_kernel,
        grid_spec=pltpu.PrefetchScalarGridSpec(
            num_scalar_prefetch=1,
            grid=(cores,),
            in_specs=[
                pl.BlockSpec((members, 1, depth, count), lambda o, at: (0, (o + at[0]) % NC, 0, 0)),
                pl.BlockSpec((members, NZ, LANES), lambda o, at: (0, count // NZ, (o + at[0]) % NC)),
            ],
            out_specs=pl.BlockSpec((1, members, depth, count), lambda o, at: (o, 0, 0, 0)),
        ),
        out_shape=jax.ShapeDtypeStruct((cores, members, depth, count), BF16),
        compiler_params=params(60),
        cost_estimate=pl.CostEstimate(
            flops=2 * cores * members * depth * LANES * (NZ + count),
            bytes_accessed=4 * cores * members * depth * count,
            transcendentals=0,
        ),
        name="mask_features",
    )(place, features, parts)


def grad_kernel(scale, feat_ref, own_ref, other_ref, out_ref):
    total = 0.0
    for o, errors in enumerate((own_ref, other_ref)):
        features = jnp.concatenate([feat_ref[o, y] for y in range(feat_ref.shape[1])], axis=1)
        total += jnp.dot(features, errors[...], preferred_element_type=F32)
    out_ref[...] = (total * scale).astype(BF16)


def grad_parts(features, own, other, scale):
    cores, members, depth, count = features.shape
    both, width = own.shape
    step = depth // 2
    return pl.pallas_call(
        functools.partial(grad_kernel, scale),
        grid=(depth // step,),
        in_specs=[
            pl.BlockSpec((cores, members, step, count), lambda i: (0, 0, i, 0)),
            pl.BlockSpec((both, width), lambda i: (0, 0)),
            pl.BlockSpec((both, width), lambda i: (0, 0)),
        ],
        out_specs=pl.BlockSpec((step, width), lambda i: (i, 0)),
        out_shape=jax.ShapeDtypeStruct((depth, width), BF16),
        compiler_params=params(60),
        cost_estimate=pl.CostEstimate(
            flops=2 * depth * cores * both * width,
            bytes_accessed=2 * (cores * both * (depth + width) + depth * width),
            transcendentals=0,
        ),
        name="grad_parts",
    )(features, own, other)


def back_kernel(y_ref, err_ref, own_ref, other_ref, *outs_and_rows):
    outs, rows = outs_and_rows[:-1], outs_and_rows[-1]
    count = err_ref.shape[0] // NY
    for o, packed in enumerate((own_ref, other_ref)):
        unpack_rows(packed, rows.at[o])
    places = {(0, 0): (0, 0), (0, 1): (0, 1), (1, 0): (1, 0), (1, 1): (1, 1)}
    places |= {(2, 0): (1, 2), (2, 1): (2, 2), (3, 0): (2, 0), (3, 1): (2, 1)}
    for d in range(NY):
        at = pl.multiple_of((y_ref[0] + d) % NY * count, count)
        for o in range(NC):
            out, k = places[d, o]
            outs[out][k] = lax.dot_general(
                rows[o].reshape(-1, rows.shape[4]),
                err_ref[pl.ds(at, count), :],
                (((1,), (1,)), ((), ())),
                preferred_element_type=F32,
            ).astype(BF16)


def back_parts(y, errors, own, other):
    shards, block, _ = own.shape
    both, width = errors.shape
    part = block // (NX * width // LANES + 1)
    depth, count = NX * shards * part, both // NY
    return pl.pallas_call(
        back_kernel,
        in_specs=[pl.BlockSpec(memory_space=pltpu.SMEM)] + [pl.BlockSpec(memory_space=pltpu.VMEM)] * 3,
        out_shape=[jax.ShapeDtypeStruct((k, depth, count), BF16) for k in (NC, NC + 1, NC + 1)],
        scratch_shapes=[pltpu.VMEM((NC, NX, shards, part, width), BF16)],
        compiler_params=params(40),
        cost_estimate=pl.CostEstimate(
            flops=2 * NC * depth * both * width,
            bytes_accessed=2 * NC * depth * (both + width),
            transcendentals=0,
        ),
        name="back_parts",
    )(y, errors, own, other)


def place_kernel(place_ref, stay_ref, up_ref, down_ref, far_up_ref, far_down_ref, out_ref, turned):
    y, c = place_ref[0] // NC, place_ref[0] % NC
    parts = {(0, 0): (stay_ref, 0), (0, 1): (stay_ref, 1), (1, 0): (up_ref, 0), (1, 1): (up_ref, 1)}
    parts |= {(2, 0): (far_up_ref, 0), (2, 1): (far_down_ref, 0), (3, 0): (down_ref, 0), (3, 1): (down_ref, 1)}
    for (d, o), (ref, k) in parts.items():
        s = (y + NY - d) % NY * NC + (c + o) % NC
        turned[:, :, pl.ds(s, 1)] = ref[k].swapaxes(0, 1)[:, :, None]
    shards, bands, shares, part, count = turned.shape
    rows = bands * shares * part
    for j in range(shards):
        out_ref[:, j * rows : (j + 1) * rows] = turned[j].reshape(rows, count).T


def place_back(place, parts):
    _, depth, count = parts[0].shape
    part = depth // (NX * NZ)
    step = NZ // 2
    columns = step * NX * GROUP * part
    return pl.pallas_call(
        place_kernel,
        grid=(NZ // step,),
        in_specs=[pl.BlockSpec(memory_space=pltpu.SMEM)]
        + [pl.BlockSpec((p.shape[0], NX, step, part, count), lambda j: (0, 0, j, 0, 0)) for p in parts],
        out_specs=pl.BlockSpec((count, columns), lambda j: (0, j)),
        out_shape=jax.ShapeDtypeStruct((count, NZ // step * columns), BF16),
        scratch_shapes=[pltpu.VMEM((step, NX, GROUP, part, count), BF16)],
        compiler_params=params(40),
        cost_estimate=pl.CostEstimate(
            flops=0, bytes_accessed=4 * NY * NC * depth * count, transcendentals=0
        ),
        name="place_back",
    )(place, *[p.reshape(p.shape[0], NX, NZ, part, count) for p in parts])


def sum_kernel(parts_ref, out_ref):
    out_ref[...] = jnp.sum(parts_ref[...].astype(F32), axis=0).astype(BF16)


def sum_parts(parts, kernel, shape, name):
    return pl.pallas_call(
        kernel,
        out_shape=jax.ShapeDtypeStruct(shape, BF16),
        compiler_params=params(40),
        name=name,
    )(parts)


def copy_kernel(parts_ref, out_ref):
    total = jnp.sum(parts_ref[...].astype(F32), axis=0).astype(BF16)
    out_ref[...] = jnp.broadcast_to(total[None], out_ref.shape)


def finish_kernel(bounds_ref, sums_ref, out_ref, owned_ref, wide):
    sums = sums_ref[...]
    out_ref[...] = sums
    wide[...] = sums.astype(F32)
    slots = owned_ref.shape[0]
    depth, width = wide.shape
    for s in range(slots):
        tile = bounds_ref[0] + s
        at = pl.multiple_of(jnp.minimum(tile, depth // TILE_ROWS - 1) * TILE_ROWS, TILE_ROWS)
        rows = jnp.where(tile < bounds_ref[1], wide[pl.ds(at, TILE_ROWS), :], 0.0)
        for r in range(TILE_ROWS):
            owned_ref[s : s + 1, r * width : (r + 1) * width] = rows[r : r + 1, :]


def finish(bounds, sums):
    depth, width = sums.shape
    slots = 3 * depth // (2 * TILE_ROWS * OWNERS)
    return pl.pallas_call(
        finish_kernel,
        in_specs=[pl.BlockSpec(memory_space=pltpu.SMEM), pl.BlockSpec(memory_space=pltpu.VMEM)],
        out_shape=[
            jax.ShapeDtypeStruct(sums.shape, BF16),
            jax.ShapeDtypeStruct((slots, TILE_ROWS * width), F32),
        ],
        scratch_shapes=[pltpu.VMEM((depth, width), F32)],
        compiler_params=params(40),
        name="finish",
    )(bounds, sums)


def exchange(parts, axes):
    return lax.all_to_all(parts, axes, split_axis=0, concat_axis=0, tiled=True)


def body(tokens, weight, target, bounds, kept):
    count, model = tokens.shape
    shard_rows, width = weight.shape
    tiles = shard_rows // TILE_ROWS
    scale = 1.0 / math.sqrt(count * NZ * OWNERS)
    part = shard_rows // OWNERS
    group = ("y", "c")
    place = lax.axis_index(group).reshape(1)
    core = lax.axis_index("c").reshape(1)
    y = lax.axis_index("y").reshape(1)
    swap = [(0, 1), (1, 0)]

    cut, packed = cut_tokens(place, tokens, weight, kept.reshape(-1))
    features = exchange(cut, group).reshape(NY, NC, model // GROUP, count)
    packed = lax.all_gather(packed, "z", axis=0, tiled=False)

    other = forward_parts(1 - core, features, packed, BF16, NZ, "forward_other")
    got = lax.ppermute(other, "c", swap)
    own = forward_parts(core, features, packed, F32, 0, "forward_own")
    outputs = exchange(join_parts(core, own, got, packed), "y")
    own = exchange(sum_errors(outputs, target), "y").reshape(-1, width)
    masked = mask_features(place, features, outputs)
    masked, packed = lax.optimization_barrier((masked, packed))
    turned = lax.ppermute(packed, "c", swap)
    own, masked = lax.optimization_barrier((own, masked))
    other = lax.ppermute(own, "c", swap)

    parts = grad_parts(masked, own, other, scale)
    parts, own = lax.optimization_barrier((parts, own))
    parts = exchange(parts.reshape(NX, NZ, part, width), "x")

    up, down = [(k, (k + 1) % NY) for k in range(NY)], [(k, (k + NY - 1) % NY) for k in range(NY)]
    stay, to_up, to_down = back_parts(y, own, packed, turned)
    parts, _, _ = lax.optimization_barrier((parts, to_up, to_down))
    from_down = lax.ppermute(to_up, "y", up)
    from_up = lax.ppermute(to_down, "y", down)
    far_down = lax.ppermute(from_down[NC:], "y", up)
    far_up = lax.ppermute(from_up[NC:], "y", down)

    parts = exchange(sum_parts(parts, sum_kernel, (NZ, part, width), "sum_x"), "z")
    parts, *_ = lax.optimization_barrier((parts, from_down, from_up))
    inputs_grad = place_back(place, [stay, from_down, from_up, far_down, far_up])
    parts = sum_parts(parts, copy_kernel, (OWNERS, part, width), "sum_z")
    selected = exchange(parts, ("x", *group)).reshape(shard_rows, width)

    selected, owned = finish(bounds.reshape(-1), selected)
    return inputs_grad, selected, owned[None, None]


def solution(mesh):
    fine = Mesh(mesh.devices.reshape(NX, NY, NC, NZ), ("x", "y", "c", "z"))
    dp = ("x", "y", "c")
    return jax.shard_map(
        body,
        mesh=fine,
        in_specs=(
            P((*dp, "z"), None),
            P("z", None),
            P((*dp, "z"), None),
            P("z", dp, None),
            P(dp, "z", None),
        ),
        out_specs=(P((*dp, "z"), None), P("z", None), P("z", dp, None, None)),
        check_vma=False,
    )
```

```python
import functools
import math

import jax
import jax.numpy as jnp
from jax import lax
from jax.experimental import pallas as pl
from jax.experimental.pallas import tpu as pltpu
from jax.sharding import Mesh, PartitionSpec as P

TILE_ROWS = 8
NX, NY, NC, NZ = 4, 4, 2, 16
GROUP = NY * NC
OWNERS = NX * GROUP
F32, BF16 = jnp.float32, jnp.bfloat16
VMEM_MB = 1024 * 1024
LANES = 128


def params(megabytes):
    return pltpu.CompilerParams(vmem_limit_bytes=megabytes * VMEM_MB)


def cut_kernel(place_ref, tok_ref, weight_ref, kept_ref, out_ref, packed_ref):
    shares, bands, shards, part, count = out_ref.shape
    rows = bands * shares * part
    for j in range(shards):
        turned = tok_ref[:, j * rows : (j + 1) * rows].T
        out_ref[:, :, j] = turned.reshape(bands, shares, part, count).swapaxes(0, 1)

    @pl.when(pl.program_id(0) == 0)
    def _():
        rows = bands * part
        blocks = weight_ref.shape[3] // LANES
        for b in range(blocks):
            block = weight_ref[:, 0, :, b * LANES : (b + 1) * LANES]
            packed_ref[b * rows : (b + 1) * rows] = block.reshape(rows, LANES)
        lane = lax.broadcasted_iota(jnp.int32, (part, LANES), 1)
        hits = jnp.zeros((part, LANES), F32)
        for k in range(kept_ref.shape[0]):
            hits = jnp.where(lane == kept_ref[k], 1.0, hits)
        first = lax.broadcasted_iota(jnp.int32, (part, LANES), 0) == 0
        packed_ref[blocks * rows :] = jnp.where(first, hits, 0.0).astype(BF16)


def cut_tokens(place, tokens, weight, kept):
    count, model = tokens.shape
    rows = model // NZ
    part = rows // OWNERS
    width = weight.shape[1]
    packed = (NX * width // LANES + 1) * part
    step = NZ // 2
    return pl.pallas_call(
        cut_kernel,
        grid_spec=pltpu.PrefetchScalarGridSpec(
            num_scalar_prefetch=1,
            grid=(NZ // step,),
            in_specs=[
                pl.BlockSpec((count, rows * step), lambda j, at: (0, j)),
                pl.BlockSpec((NX, 1, part, width), lambda j, at: (0, at[0], 0, 0)),
                pl.BlockSpec(memory_space=pltpu.SMEM),
            ],
            out_specs=[
                pl.BlockSpec((GROUP, NX, step, part, count), lambda j, at: (0, 0, j, 0, 0)),
                pl.BlockSpec((packed, LANES), lambda j, at: (0, 0)),
            ],
        ),
        out_shape=[
            jax.ShapeDtypeStruct((GROUP, NX, NZ, part, count), BF16),
            jax.ShapeDtypeStruct((packed, LANES), BF16),
        ],
        compiler_params=params(60),
        cost_estimate=pl.CostEstimate(flops=0, bytes_accessed=4 * count * model, transcendentals=0),
        name="cut_tokens",
    )(place, tokens, weight.reshape(NX, GROUP, part, width), kept)


def unpack_rows(packed_ref, rows):
    bands, _, part, width = rows.shape
    for b in range(width // LANES):
        for x in range(bands):
            at = (b * bands + x) * part
            rows[x, :, :, b * LANES : (b + 1) * LANES] = packed_ref[:, at : at + part, :]


def forward_kernel(core_ref, feat_ref, packed_ref, out_ref, rows):
    width = rows.shape[3]
    count = feat_ref.shape[3]

    @pl.when(pl.program_id(0) == 0)
    def _():
        unpack_rows(packed_ref, rows)

    out_ref[0, :count] = lax.dot_general(
        feat_ref[0, 0],
        rows[...].reshape(-1, width),
        (((0,), (0,)), ((), ())),
        preferred_element_type=F32,
    ).astype(out_ref.dtype)
    if out_ref.shape[1] > count:
        out_ref[0, count:] = jnp.zeros((out_ref.shape[1] - count, width), BF16)
        out_ref[0, count:, :LANES] = read_hits(packed_ref[:, NX * rows.shape[2] * width // LANES :, :])


def read_hits(block):
    return jnp.sum(block.astype(F32), axis=1).astype(BF16)


def forward_parts(core, features, packed, kind, extra, name):
    members, _, depth, count = features.shape
    shards, block, _ = packed.shape
    part = depth // (NX * shards)
    width = (block // part - 1) // NX * LANES
    return pl.pallas_call(
        forward_kernel,
        grid_spec=pltpu.PrefetchScalarGridSpec(
            num_scalar_prefetch=1,
            grid=(members,),
            in_specs=[
                pl.BlockSpec((1, 1, depth, count), lambda i, at: (i, at[0], 0, 0)),
                pl.BlockSpec((shards, block, LANES), lambda i, at: (0, 0, 0)),
            ],
            out_specs=pl.BlockSpec((1, count + extra, width), lambda i, at: (i, 0, 0)),
            scratch_shapes=[pltpu.VMEM((NX, shards, part, width), BF16)],
        ),
        out_shape=jax.ShapeDtypeStruct((members, count + extra, width), kind),
        compiler_params=params(40),
        cost_estimate=pl.CostEstimate(
            flops=2 * members * depth * count * width,
            bytes_accessed=2 * (members * count * (depth + width) + depth * width),
            transcendentals=0,
        ),
        name=name,
    )(core, features, packed)


def join_kernel(core_ref, own_ref, got_ref, packed_ref, out_ref):
    count = own_ref.shape[1]
    shards = packed_ref.shape[0]
    out_ref[:, :count] = (own_ref[...] + got_ref[:, :count, :].astype(F32)).astype(BF16)
    mine = read_hits(packed_ref[...]).astype(F32)
    other = got_ref[0, count:, :LANES].astype(F32)
    members, _, width = got_ref.shape
    out_ref[:, count:] = jnp.zeros((members, shards, width), BF16)
    for c in range(NC):
        hits = jnp.where(core_ref[0] == c, mine, other).astype(BF16)
        out_ref[:, count:, c * LANES : (c + 1) * LANES] = jnp.broadcast_to(hits[None], (members, shards, LANES))


def join_parts(core, own, got, packed):
    members, count, width = own.shape
    shards, block, _ = packed.shape
    part = got.shape[1] - count
    return pl.pallas_call(
        join_kernel,
        grid=(1,),
        in_specs=[
            pl.BlockSpec(memory_space=pltpu.SMEM),
            pl.BlockSpec(own.shape, lambda i: (0, 0, 0)),
            pl.BlockSpec(got.shape, lambda i: (0, 0, 0)),
            pl.BlockSpec((shards, part, LANES), lambda i: (0, block // part - 1, 0)),
        ],
        out_specs=pl.BlockSpec((members, count + shards, width), lambda i: (0, 0, 0)),
        out_shape=jax.ShapeDtypeStruct((members, count + shards, width), BF16),
        compiler_params=params(40),
        name="join_parts",
    )(core, own, got, packed)


def error_kernel(parts_ref, target_ref, copies_ref):
    count = target_ref.shape[0]
    outputs = jnp.sum(parts_ref[:, :count, :].astype(F32), axis=0)
    errors = (outputs - target_ref[...].astype(F32)).astype(BF16)
    copies_ref[...] = jnp.broadcast_to(errors[None], copies_ref.shape)


def sum_errors(parts, target):
    return pl.pallas_call(
        error_kernel,
        out_shape=jax.ShapeDtypeStruct((parts.shape[0], *target.shape), BF16),
        compiler_params=params(40),
        name="sum_errors",
    )(parts, target)


def mask_kernel(place_ref, feat_ref, hits_ref, out_ref):
    members, _, depth, count = feat_ref.shape
    shards, lanes = hits_ref.shape[1:]
    part = depth // (NX * shards)
    each = part // TILE_ROWS
    row = lax.broadcasted_iota(jnp.int32, (depth, shards), 0)
    at = lax.broadcasted_iota(jnp.int32, (depth, shards), 1)
    shard = ((row // part) % shards == at).astype(BF16)
    row = lax.broadcasted_iota(jnp.int32, (depth, lanes), 0)
    at = lax.broadcasted_iota(jnp.int32, (depth, lanes), 1)
    tile = (row // (part * shards) * GROUP + place_ref[0]) * each + row // TILE_ROWS % each
    ones = jnp.ones((lanes, count), BF16)
    for y in range(members):
        hits = jnp.dot(shard, hits_ref[y], preferred_element_type=F32)
        hits = jnp.where(tile == at, hits, 0.0).astype(BF16)
        keep = jnp.dot(hits, ones, preferred_element_type=F32)
        out_ref[0, y] = feat_ref[y, 0] * keep.astype(BF16)


def mask_features(place, features, parts):
    members, cores, depth, count = features.shape
    return pl.pallas_call(
        mask_kernel,
        grid_spec=pltpu.PrefetchScalarGridSpec(
            num_scalar_prefetch=1,
            grid=(cores,),
            in_specs=[
                pl.BlockSpec((members, 1, depth, count), lambda o, at: (0, (o + at[0]) % NC, 0, 0)),
                pl.BlockSpec((members, NZ, LANES), lambda o, at: (0, count // NZ, (o + at[0]) % NC)),
            ],
            out_specs=pl.BlockSpec((1, members, depth, count), lambda o, at: (o, 0, 0, 0)),
        ),
        out_shape=jax.ShapeDtypeStruct((cores, members, depth, count), BF16),
        compiler_params=params(60),
        cost_estimate=pl.CostEstimate(
            flops=2 * cores * members * depth * LANES * (NZ + count),
            bytes_accessed=4 * cores * members * depth * count,
            transcendentals=0,
        ),
        name="mask_features",
    )(place, features, parts)


def grad_kernel(scale, feat_ref, own_ref, other_ref, out_ref):
    total = 0.0
    for o, errors in enumerate((own_ref, other_ref)):
        features = jnp.concatenate([feat_ref[o, y] for y in range(feat_ref.shape[1])], axis=1)
        total += jnp.dot(features, errors[...], preferred_element_type=F32)
    out_ref[...] = (total * scale).astype(BF16)


def grad_parts(features, own, other, scale):
    cores, members, depth, count = features.shape
    both, width = own.shape
    step = depth // 2
    return pl.pallas_call(
        functools.partial(grad_kernel, scale),
        grid=(depth // step,),
        in_specs=[
            pl.BlockSpec((cores, members, step, count), lambda i: (0, 0, i, 0)),
            pl.BlockSpec((both, width), lambda i: (0, 0)),
            pl.BlockSpec((both, width), lambda i: (0, 0)),
        ],
        out_specs=pl.BlockSpec((step, width), lambda i: (i, 0)),
        out_shape=jax.ShapeDtypeStruct((depth, width), BF16),
        compiler_params=params(60),
        cost_estimate=pl.CostEstimate(
            flops=2 * depth * cores * both * width,
            bytes_accessed=2 * (cores * both * (depth + width) + depth * width),
            transcendentals=0,
        ),
        name="grad_parts",
    )(features, own, other)


def back_kernel(y_ref, err_ref, own_ref, other_ref, *outs_and_rows):
    outs, rows = outs_and_rows[:-1], outs_and_rows[-1]
    count = err_ref.shape[0] // NY
    for o, packed in enumerate((own_ref, other_ref)):
        unpack_rows(packed, rows.at[o])
    places = {(0, 0): (0, 0), (0, 1): (0, 1), (1, 0): (1, 0), (1, 1): (1, 1)}
    places |= {(2, 0): (1, 2), (2, 1): (2, 2), (3, 0): (2, 0), (3, 1): (2, 1)}
    for d in range(NY):
        at = pl.multiple_of((y_ref[0] + d) % NY * count, count)
        for o in range(NC):
            out, k = places[d, o]
            outs[out][k] = lax.dot_general(
                rows[o].reshape(-1, rows.shape[4]),
                err_ref[pl.ds(at, count), :],
                (((1,), (1,)), ((), ())),
                preferred_element_type=F32,
            ).astype(BF16)


def back_parts(y, errors, own, other):
    shards, block, _ = own.shape
    both, width = errors.shape
    part = block // (NX * width // LANES + 1)
    depth, count = NX * shards * part, both // NY
    return pl.pallas_call(
        back_kernel,
        in_specs=[pl.BlockSpec(memory_space=pltpu.SMEM)] + [pl.BlockSpec(memory_space=pltpu.VMEM)] * 3,
        out_shape=[jax.ShapeDtypeStruct((k, depth, count), BF16) for k in (NC, NC + 1, NC + 1)],
        scratch_shapes=[pltpu.VMEM((NC, NX, shards, part, width), BF16)],
        compiler_params=params(40),
        cost_estimate=pl.CostEstimate(
            flops=2 * NC * depth * both * width,
            bytes_accessed=2 * NC * depth * (both + width),
            transcendentals=0,
        ),
        name="back_parts",
    )(y, errors, own, other)


def place_kernel(place_ref, stay_ref, up_ref, down_ref, far_up_ref, far_down_ref, out_ref, turned):
    y, c = place_ref[0] // NC, place_ref[0] % NC
    parts = {(0, 0): (stay_ref, 0), (0, 1): (stay_ref, 1), (1, 0): (up_ref, 0), (1, 1): (up_ref, 1)}
    parts |= {(2, 0): (far_up_ref, 0), (2, 1): (far_down_ref, 0), (3, 0): (down_ref, 0), (3, 1): (down_ref, 1)}
    for (d, o), (ref, k) in parts.items():
        s = (y + NY - d) % NY * NC + (c + o) % NC
        turned[:, :, pl.ds(s, 1)] = ref[k].swapaxes(0, 1)[:, :, None]
    shards, bands, shares, part, count = turned.shape
    rows = bands * shares * part
    for j in range(shards):
        out_ref[:, j * rows : (j + 1) * rows] = turned[j].reshape(rows, count).T


def place_back(place, parts):
    _, depth, count = parts[0].shape
    part = depth // (NX * NZ)
    step = NZ // 2
    columns = step * NX * GROUP * part
    return pl.pallas_call(
        place_kernel,
        grid=(NZ // step,),
        in_specs=[pl.BlockSpec(memory_space=pltpu.SMEM)]
        + [pl.BlockSpec((p.shape[0], NX, step, part, count), lambda j: (0, 0, j, 0, 0)) for p in parts],
        out_specs=pl.BlockSpec((count, columns), lambda j: (0, j)),
        out_shape=jax.ShapeDtypeStruct((count, NZ // step * columns), BF16),
        scratch_shapes=[pltpu.VMEM((step, NX, GROUP, part, count), BF16)],
        compiler_params=params(40),
        cost_estimate=pl.CostEstimate(
            flops=0, bytes_accessed=4 * NY * NC * depth * count, transcendentals=0
        ),
        name="place_back",
    )(place, *[p.reshape(p.shape[0], NX, NZ, part, count) for p in parts])


def sum_kernel(parts_ref, out_ref):
    out_ref[...] = jnp.sum(parts_ref[...].astype(F32), axis=0).astype(BF16)


def sum_parts(parts, kernel, shape, name):
    return pl.pallas_call(
        kernel,
        out_shape=jax.ShapeDtypeStruct(shape, BF16),
        compiler_params=params(40),
        name=name,
    )(parts)


def copy_kernel(parts_ref, out_ref):
    total = jnp.sum(parts_ref[...].astype(F32), axis=0).astype(BF16)
    out_ref[...] = jnp.broadcast_to(total[None], out_ref.shape)


def exchange(parts, axes):
    return lax.all_to_all(parts, axes, split_axis=0, concat_axis=0, tiled=True)


def body(tokens, weight, target, bounds, kept):
    count, model = tokens.shape
    shard_rows, width = weight.shape
    tiles = shard_rows // TILE_ROWS
    scale = 1.0 / math.sqrt(count * NZ * OWNERS)
    part = shard_rows // OWNERS
    group = ("y", "c")
    place = lax.axis_index(group).reshape(1)
    core = lax.axis_index("c").reshape(1)
    y = lax.axis_index("y").reshape(1)
    swap = [(0, 1), (1, 0)]

    cut, packed = cut_tokens(place, tokens, weight, kept.reshape(-1))
    features = exchange(cut, group).reshape(NY, NC, model // GROUP, count)
    packed = lax.all_gather(packed, "z", axis=0, tiled=False)

    other = forward_parts(1 - core, features, packed, BF16, NZ, "forward_other")
    got = lax.ppermute(other, "c", swap)
    own = forward_parts(core, features, packed, F32, 0, "forward_own")
    outputs = exchange(join_parts(core, own, got, packed), "y")
    own = exchange(sum_errors(outputs, target), "y").reshape(-1, width)
    masked = mask_features(place, features, outputs)
    masked, packed = lax.optimization_barrier((masked, packed))
    turned = lax.ppermute(packed, "c", swap)
    own, masked = lax.optimization_barrier((own, masked))
    other = lax.ppermute(own, "c", swap)

    parts = grad_parts(masked, own, other, scale)
    parts, own = lax.optimization_barrier((parts, own))
    parts = exchange(parts.reshape(NX, NZ, part, width), "x")

    up, down = [(k, (k + 1) % NY) for k in range(NY)], [(k, (k + NY - 1) % NY) for k in range(NY)]
    stay, to_up, to_down = back_parts(y, own, packed, turned)
    parts, _, _ = lax.optimization_barrier((parts, to_up, to_down))
    from_down = lax.ppermute(to_up, "y", up)
    from_up = lax.ppermute(to_down, "y", down)
    far_down = lax.ppermute(from_down[NC:], "y", up)
    far_up = lax.ppermute(from_up[NC:], "y", down)

    parts = exchange(sum_parts(parts, sum_kernel, (NZ, part, width), "sum_x"), "z")
    parts, *_ = lax.optimization_barrier((parts, far_down, from_up))
    inputs_grad = place_back(place, [stay, from_down, from_up, far_down, far_up])
    parts = sum_parts(parts, copy_kernel, (OWNERS, part, width), "sum_z")
    selected = exchange(parts, ("x", *group)).reshape(shard_rows, width)

    first, last = bounds[0, 0, 0], bounds[0, 0, 1]
    slots = []
    for s in range(3 * tiles // (2 * OWNERS)):
        at = jnp.minimum(first + s, tiles - 1) * TILE_ROWS
        tile = lax.dynamic_slice_in_dim(selected, at, TILE_ROWS, 0).astype(F32)
        slots.append(jnp.where(s < last - first, tile, 0.0).reshape(-1))
    return inputs_grad, selected, jnp.stack(slots)[None, None]


def solution(mesh):
    fine = Mesh(mesh.devices.reshape(NX, NY, NC, NZ), ("x", "y", "c", "z"))
    dp = ("x", "y", "c")
    return jax.shard_map(
        body,
        mesh=fine,
        in_specs=(
            P((*dp, "z"), None),
            P("z", None),
            P((*dp, "z"), None),
            P("z", dp, None),
            P(dp, "z", None),
        ),
        out_specs=(P((*dp, "z"), None), P("z", None), P("z", dp, None, None)),
        check_vma=False,
    )
```

```python
import functools
import math

import jax
import jax.numpy as jnp
from jax import lax
from jax.experimental import pallas as pl
from jax.experimental.pallas import tpu as pltpu
from jax.sharding import Mesh, PartitionSpec as P

TILE_ROWS = 8
NX, NY, NC, NZ = 4, 4, 2, 16
GROUP = NY * NC
OWNERS = NX * GROUP
F32, BF16 = jnp.float32, jnp.bfloat16
VMEM_MB = 1024 * 1024
LANES = 128


def params(megabytes):
    return pltpu.CompilerParams(vmem_limit_bytes=megabytes * VMEM_MB)


def cut_kernel(place_ref, tok_ref, weight_ref, kept_ref, out_ref, packed_ref):
    shares, bands, shards, part, count = out_ref.shape
    rows = bands * shares * part
    for j in range(shards):
        turned = tok_ref[:, j * rows : (j + 1) * rows].T
        out_ref[:, :, j] = turned.reshape(bands, shares, part, count).swapaxes(0, 1)

    @pl.when(pl.program_id(0) == 0)
    def _():
        rows = bands * part
        blocks = weight_ref.shape[3] // LANES
        for b in range(blocks):
            block = weight_ref[:, 0, :, b * LANES : (b + 1) * LANES]
            packed_ref[b * rows : (b + 1) * rows] = block.reshape(rows, LANES)
        lane = lax.broadcasted_iota(jnp.int32, (part, LANES), 1)
        hits = jnp.zeros((part, LANES), F32)
        for k in range(kept_ref.shape[0]):
            hits = jnp.where(lane == kept_ref[k], 1.0, hits)
        first = lax.broadcasted_iota(jnp.int32, (part, LANES), 0) == 0
        packed_ref[blocks * rows :] = jnp.where(first, hits, 0.0).astype(BF16)


def cut_tokens(place, tokens, weight, kept):
    count, model = tokens.shape
    rows = model // NZ
    part = rows // OWNERS
    width = weight.shape[1]
    packed = (NX * width // LANES + 1) * part
    step = NZ // 2
    return pl.pallas_call(
        cut_kernel,
        grid_spec=pltpu.PrefetchScalarGridSpec(
            num_scalar_prefetch=1,
            grid=(NZ // step,),
            in_specs=[
                pl.BlockSpec((count, rows * step), lambda j, at: (0, j)),
                pl.BlockSpec((NX, 1, part, width), lambda j, at: (0, at[0], 0, 0)),
                pl.BlockSpec(memory_space=pltpu.SMEM),
            ],
            out_specs=[
                pl.BlockSpec((GROUP, NX, step, part, count), lambda j, at: (0, 0, j, 0, 0)),
                pl.BlockSpec((packed, LANES), lambda j, at: (0, 0)),
            ],
        ),
        out_shape=[
            jax.ShapeDtypeStruct((GROUP, NX, NZ, part, count), BF16),
            jax.ShapeDtypeStruct((packed, LANES), BF16),
        ],
        compiler_params=params(60),
        cost_estimate=pl.CostEstimate(flops=0, bytes_accessed=4 * count * model, transcendentals=0),
        name="cut_tokens",
    )(place, tokens, weight.reshape(NX, GROUP, part, width), kept)


def unpack_rows(packed_ref, rows):
    bands, _, part, width = rows.shape
    for b in range(width // LANES):
        for x in range(bands):
            at = (b * bands + x) * part
            rows[x, :, :, b * LANES : (b + 1) * LANES] = packed_ref[:, at : at + part, :]


def forward_kernel(core_ref, feat_ref, packed_ref, out_ref, rows):
    width = rows.shape[3]
    count = feat_ref.shape[3]

    @pl.when(pl.program_id(0) == 0)
    def _():
        unpack_rows(packed_ref, rows)

    out_ref[0, :count] = lax.dot_general(
        feat_ref[0, 0],
        rows[...].reshape(-1, width),
        (((0,), (0,)), ((), ())),
        preferred_element_type=F32,
    ).astype(out_ref.dtype)
    if out_ref.shape[1] > count:
        out_ref[0, count:] = jnp.zeros((out_ref.shape[1] - count, width), BF16)
        out_ref[0, count:, :LANES] = read_hits(packed_ref[:, NX * rows.shape[2] * width // LANES :, :])


def read_hits(block):
    return jnp.sum(block.astype(F32), axis=1).astype(BF16)


def forward_parts(core, features, packed, kind, extra, name):
    members, _, depth, count = features.shape
    shards, block, _ = packed.shape
    part = depth // (NX * shards)
    width = (block // part - 1) // NX * LANES
    return pl.pallas_call(
        forward_kernel,
        grid_spec=pltpu.PrefetchScalarGridSpec(
            num_scalar_prefetch=1,
            grid=(members,),
            in_specs=[
                pl.BlockSpec((1, 1, depth, count), lambda i, at: (i, at[0], 0, 0)),
                pl.BlockSpec((shards, block, LANES), lambda i, at: (0, 0, 0)),
            ],
            out_specs=pl.BlockSpec((1, count + extra, width), lambda i, at: (i, 0, 0)),
            scratch_shapes=[pltpu.VMEM((NX, shards, part, width), BF16)],
        ),
        out_shape=jax.ShapeDtypeStruct((members, count + extra, width), kind),
        compiler_params=params(40),
        cost_estimate=pl.CostEstimate(
            flops=2 * members * depth * count * width,
            bytes_accessed=2 * (members * count * (depth + width) + depth * width),
            transcendentals=0,
        ),
        name=name,
    )(core, features, packed)


def join_kernel(core_ref, own_ref, got_ref, packed_ref, out_ref):
    count = own_ref.shape[1]
    shards = packed_ref.shape[0]
    out_ref[:, :count] = (own_ref[...] + got_ref[:, :count, :].astype(F32)).astype(BF16)
    mine = read_hits(packed_ref[...]).astype(F32)
    other = got_ref[0, count:, :LANES].astype(F32)
    members, _, width = got_ref.shape
    out_ref[:, count:] = jnp.zeros((members, shards, width), BF16)
    for c in range(NC):
        hits = jnp.where(core_ref[0] == c, mine, other).astype(BF16)
        out_ref[:, count:, c * LANES : (c + 1) * LANES] = jnp.broadcast_to(hits[None], (members, shards, LANES))


def join_parts(core, own, got, packed):
    members, count, width = own.shape
    shards, block, _ = packed.shape
    part = got.shape[1] - count
    return pl.pallas_call(
        join_kernel,
        grid=(1,),
        in_specs=[
            pl.BlockSpec(memory_space=pltpu.SMEM),
            pl.BlockSpec(own.shape, lambda i: (0, 0, 0)),
            pl.BlockSpec(got.shape, lambda i: (0, 0, 0)),
            pl.BlockSpec((shards, part, LANES), lambda i: (0, block // part - 1, 0)),
        ],
        out_specs=pl.BlockSpec((members, count + shards, width), lambda i: (0, 0, 0)),
        out_shape=jax.ShapeDtypeStruct((members, count + shards, width), BF16),
        compiler_params=params(40),
        name="join_parts",
    )(core, own, got, packed)


def error_kernel(parts_ref, target_ref, copies_ref):
    count = target_ref.shape[0]
    outputs = jnp.sum(parts_ref[:, :count, :].astype(F32), axis=0)
    errors = (outputs - target_ref[...].astype(F32)).astype(BF16)
    copies_ref[...] = jnp.broadcast_to(errors[None], copies_ref.shape)


def sum_errors(parts, target):
    return pl.pallas_call(
        error_kernel,
        out_shape=jax.ShapeDtypeStruct((parts.shape[0], *target.shape), BF16),
        compiler_params=params(40),
        name="sum_errors",
    )(parts, target)


def mask_kernel(place_ref, feat_ref, hits_ref, out_ref):
    members, _, depth, count = feat_ref.shape
    shards, lanes = hits_ref.shape[1:]
    part = depth // (NX * shards)
    each = part // TILE_ROWS
    row = lax.broadcasted_iota(jnp.int32, (depth, shards), 0)
    at = lax.broadcasted_iota(jnp.int32, (depth, shards), 1)
    shard = ((row // part) % shards == at).astype(BF16)
    row = lax.broadcasted_iota(jnp.int32, (depth, lanes), 0)
    at = lax.broadcasted_iota(jnp.int32, (depth, lanes), 1)
    tile = (row // (part * shards) * GROUP + place_ref[0]) * each + row // TILE_ROWS % each
    ones = jnp.ones((lanes, count), BF16)
    for y in range(members):
        hits = jnp.dot(shard, hits_ref[y], preferred_element_type=F32)
        hits = jnp.where(tile == at, hits, 0.0).astype(BF16)
        keep = jnp.dot(hits, ones, preferred_element_type=F32)
        out_ref[0, y] = feat_ref[y, 0] * keep.astype(BF16)


def mask_features(place, features, parts):
    members, cores, depth, count = features.shape
    return pl.pallas_call(
        mask_kernel,
        grid_spec=pltpu.PrefetchScalarGridSpec(
            num_scalar_prefetch=1,
            grid=(cores,),
            in_specs=[
                pl.BlockSpec((members, 1, depth, count), lambda o, at: (0, (o + at[0]) % NC, 0, 0)),
                pl.BlockSpec((members, NZ, LANES), lambda o, at: (0, count // NZ, (o + at[0]) % NC)),
            ],
            out_specs=pl.BlockSpec((1, members, depth, count), lambda o, at: (o, 0, 0, 0)),
        ),
        out_shape=jax.ShapeDtypeStruct((cores, members, depth, count), BF16),
        compiler_params=params(60),
        cost_estimate=pl.CostEstimate(
            flops=2 * cores * members * depth * LANES * (NZ + count),
            bytes_accessed=4 * cores * members * depth * count,
            transcendentals=0,
        ),
        name="mask_features",
    )(place, features, parts)


def grad_kernel(scale, feat_ref, own_ref, other_ref, out_ref):
    total = 0.0
    for o, errors in enumerate((own_ref, other_ref)):
        features = jnp.concatenate([feat_ref[o, y] for y in range(feat_ref.shape[1])], axis=1)
        total += jnp.dot(features, errors[...], preferred_element_type=F32)
    out_ref[...] = (total * scale).astype(BF16)


def grad_parts(features, own, other, scale):
    cores, members, depth, count = features.shape
    both, width = own.shape
    step = depth // 2
    return pl.pallas_call(
        functools.partial(grad_kernel, scale),
        grid=(depth // step,),
        in_specs=[
            pl.BlockSpec((cores, members, step, count), lambda i: (0, 0, i, 0)),
            pl.BlockSpec((both, width), lambda i: (0, 0)),
            pl.BlockSpec((both, width), lambda i: (0, 0)),
        ],
        out_specs=pl.BlockSpec((step, width), lambda i: (i, 0)),
        out_shape=jax.ShapeDtypeStruct((depth, width), BF16),
        compiler_params=params(60),
        cost_estimate=pl.CostEstimate(
            flops=2 * depth * cores * both * width,
            bytes_accessed=2 * (cores * both * (depth + width) + depth * width),
            transcendentals=0,
        ),
        name="grad_parts",
    )(features, own, other)


def back_kernel(y_ref, err_ref, own_ref, other_ref, *outs_and_rows):
    outs, rows = outs_and_rows[:-1], outs_and_rows[-1]
    count = err_ref.shape[0] // NY
    for o, packed in enumerate((own_ref, other_ref)):
        unpack_rows(packed, rows.at[o])
    for d in range(NY):
        at = pl.multiple_of((y_ref[0] + d) % NY * count, count)
        for o in range(NC):
            outs[d][o] = lax.dot_general(
                rows[o].reshape(-1, rows.shape[4]),
                err_ref[pl.ds(at, count), :],
                (((1,), (1,)), ((), ())),
                preferred_element_type=F32,
            ).astype(BF16)


def back_parts(y, errors, own, other):
    shards, block, _ = own.shape
    both, width = errors.shape
    part = block // (NX * width // LANES + 1)
    depth, count = NX * shards * part, both // NY
    return pl.pallas_call(
        back_kernel,
        in_specs=[pl.BlockSpec(memory_space=pltpu.SMEM)] + [pl.BlockSpec(memory_space=pltpu.VMEM)] * 3,
        out_shape=[jax.ShapeDtypeStruct((NC, depth, count), BF16)] * NY,
        scratch_shapes=[pltpu.VMEM((NC, NX, shards, part, width), BF16)],
        compiler_params=params(40),
        cost_estimate=pl.CostEstimate(
            flops=2 * NC * depth * both * width,
            bytes_accessed=2 * NC * depth * (both + width),
            transcendentals=0,
        ),
        name="back_parts",
    )(y, errors, own, other)


def place_kernel(place_ref, *refs):
    parts, out_ref, turned = refs[:NY], refs[NY], refs[NY + 1]
    y, c = place_ref[0] // NC, place_ref[0] % NC
    for d in range(NY):
        for o in range(NC):
            s = (y + NY - d) % NY * NC + (c + o) % NC
            turned[:, :, pl.ds(s, 1)] = parts[d][o].swapaxes(0, 1)[:, :, None]
    shards, bands, shares, part, count = turned.shape
    rows = bands * shares * part
    for j in range(shards):
        out_ref[:, j * rows : (j + 1) * rows] = turned[j].reshape(rows, count).T


def place_back(place, parts):
    cores, depth, count = parts[0].shape
    part = depth // (NX * NZ)
    step = NZ // 2
    columns = step * NX * GROUP * part
    return pl.pallas_call(
        place_kernel,
        grid=(NZ // step,),
        in_specs=[pl.BlockSpec(memory_space=pltpu.SMEM)]
        + [pl.BlockSpec((cores, NX, step, part, count), lambda j: (0, 0, j, 0, 0))] * NY,
        out_specs=pl.BlockSpec((count, columns), lambda j: (0, j)),
        out_shape=jax.ShapeDtypeStruct((count, NZ // step * columns), BF16),
        scratch_shapes=[pltpu.VMEM((step, NX, GROUP, part, count), BF16)],
        compiler_params=params(40),
        cost_estimate=pl.CostEstimate(
            flops=0, bytes_accessed=4 * NY * cores * depth * count, transcendentals=0
        ),
        name="place_back",
    )(place, *[p.reshape(cores, NX, NZ, part, count) for p in parts])


def sum_kernel(parts_ref, out_ref):
    out_ref[...] = jnp.sum(parts_ref[...].astype(F32), axis=0).astype(BF16)


def sum_parts(parts, kernel, shape, name):
    return pl.pallas_call(
        kernel,
        out_shape=jax.ShapeDtypeStruct(shape, BF16),
        compiler_params=params(40),
        name=name,
    )(parts)


def copy_kernel(parts_ref, out_ref):
    total = jnp.sum(parts_ref[...].astype(F32), axis=0).astype(BF16)
    out_ref[...] = jnp.broadcast_to(total[None], out_ref.shape)


def exchange(parts, axes):
    return lax.all_to_all(parts, axes, split_axis=0, concat_axis=0, tiled=True)


def body(tokens, weight, target, bounds, kept):
    count, model = tokens.shape
    shard_rows, width = weight.shape
    tiles = shard_rows // TILE_ROWS
    scale = 1.0 / math.sqrt(count * NZ * OWNERS)
    part = shard_rows // OWNERS
    group = ("y", "c")
    place = lax.axis_index(group).reshape(1)
    core = lax.axis_index("c").reshape(1)
    y = lax.axis_index("y").reshape(1)
    swap = [(0, 1), (1, 0)]

    cut, packed = cut_tokens(place, tokens, weight, kept.reshape(-1))
    features = exchange(cut, group).reshape(NY, NC, model // GROUP, count)
    packed = lax.all_gather(packed, "z", axis=0, tiled=False)

    other = forward_parts(1 - core, features, packed, BF16, NZ, "forward_other")
    got = lax.ppermute(other, "c", swap)
    own = forward_parts(core, features, packed, F32, 0, "forward_own")
    outputs = exchange(join_parts(core, own, got, packed), "y")
    own = exchange(sum_errors(outputs, target), "y").reshape(-1, width)
    masked = mask_features(place, features, outputs)
    masked, packed = lax.optimization_barrier((masked, packed))
    turned = lax.ppermute(packed, "c", swap)
    own, masked = lax.optimization_barrier((own, masked))
    other = lax.ppermute(own, "c", swap)

    parts = grad_parts(masked, own, other, scale)
    parts, own = lax.optimization_barrier((parts, own))
    parts = exchange(parts.reshape(NX, NZ, part, width), "x")

    back = back_parts(y, own, packed, turned)
    parts, *_ = lax.optimization_barrier((parts, *back))
    back = [
        back[d] if d == 0 else lax.ppermute(back[d], "y", [(k, (k + d) % NY) for k in range(NY)])
        for d in range(NY)
    ]
    inputs_grad = place_back(place, back)

    parts = exchange(sum_parts(parts, sum_kernel, (NZ, part, width), "sum_x"), "z")
    parts = sum_parts(parts, copy_kernel, (OWNERS, part, width), "sum_z")
    selected = exchange(parts, ("x", *group)).reshape(shard_rows, width)

    first, last = bounds[0, 0, 0], bounds[0, 0, 1]
    slots = []
    for s in range(3 * tiles // (2 * OWNERS)):
        at = jnp.minimum(first + s, tiles - 1) * TILE_ROWS
        tile = lax.dynamic_slice_in_dim(selected, at, TILE_ROWS, 0).astype(F32)
        slots.append(jnp.where(s < last - first, tile, 0.0).reshape(-1))
    return inputs_grad, selected, jnp.stack(slots)[None, None]


def solution(mesh):
    fine = Mesh(mesh.devices.reshape(NX, NY, NC, NZ), ("x", "y", "c", "z"))
    dp = ("x", "y", "c")
    return jax.shard_map(
        body,
        mesh=fine,
        in_specs=(
            P((*dp, "z"), None),
            P("z", None),
            P((*dp, "z"), None),
            P("z", dp, None),
            P(dp, "z", None),
        ),
        out_specs=(P((*dp, "z"), None), P("z", None), P("z", dp, None, None)),
        check_vma=False,
    )
```
